512 devices in a mesh: dp: 8 (over z_hi, core), seq: 64 (over z_lo, x, y).
Axes of the slice: x: 4, y: 8, z: 8 (z_hi: 4, z_lo: 2; z = z_hi * 2 + z_lo), core: 2. Of those that a mesh axis runs over, the one named last changes fastest.
Arguments:
- query: bfloat16 [8, 8192, 2048], P('dp', 'seq'), may hold values from -32 to 32
- key: bfloat16 [8, 8192, 2048], P('dp', 'seq'), may hold values from -32 to 32
- value: bfloat16 [8, 8192, 2048], P('dp', 'seq'), may hold values from -12 to 12
- gains: float32 [4, 128], replicated, may hold values from 1 to 5.5
- d_mixed: bfloat16 [8, 2, 128, 32, 2048], P('dp', None, 'seq'), may hold values from -12 to 12
Outputs:
- mixed: bfloat16 [8, 2, 128, 32, 2048], P('dp', None, 'seq')
- query_grad: bfloat16 [8, 8192, 2048], P('dp', 'seq')
- key_grad: bfloat16 [8, 8192, 2048], P('dp', 'seq')
- value_grad: bfloat16 [8, 8192, 2048], P('dp', 'seq')
- gain_grads: float32 [4, 128], replicated
The draws below stay inside these ranges and needn't reach their ends.
All inputs are finite; a program needn't handle non-finite values.
Results may differ from the reference program's by a relative error of at most 0.009.
The reference program's roundings to bfloat16 on the way count: a program that leaves them out, or rounds other values in their place, can miss the bound.
Values may be sent and summed in bfloat16 or wider, within the bound.
A program may use at most 64 MiB of HBM per device.

```python
import jax
import jax.numpy as jnp
from jax import lax

HEADS = 16
HD = 128
PATCHES = 256
SPLIT = 2
FRAMES = 32
ROWS = 128
TOKENS = 8192
SAMPLES = 8
WIDTH = 2048


def shared_normal(key):
    return jnp.clip(jax.random.normal(key, (SAMPLES, TOKENS, HEADS * HD), jnp.float32), -4.0, 4.0)


def draw_key(key, part):
    shared = shared_normal(key)
    return shared.astype(jnp.bfloat16)


def draw_query(key, part):
    key = jax.random.fold_in(key, 12)
    fresh = jnp.clip(jax.random.normal(key, (SAMPLES, TOKENS, HEADS * HD), jnp.float32), -4.0, 4.0)
    return fresh.astype(jnp.bfloat16)


def draw_gains(key, part):
    key = jax.random.fold_in(key, 13)
    return jax.random.uniform(key, (4, HD), jnp.float32, 1.0, 2.0)


def shard_levels(key, extent, pieces, least, top_value):
    def one(axis_at, parts):
        steps = jax.random.uniform(jax.random.fold_in(jax.random.fold_in(key, 6), axis_at), (parts,), jnp.float32, least / len(pieces), top_value / len(pieces))
        return jnp.repeat(jnp.exp(steps), extent[axis_at] // parts).reshape((-1,) + (1,) * (len(extent) - axis_at - 1))

    level = one(*pieces[0])
    for cut in pieces[1:]:
        level = level * one(*cut)
    return level


def noise(rng, shape, deviation, bound, split=(), held_as=jnp.bfloat16):
    level = shard_levels(rng, shape, split, -0.22, 0.18) if split else 1.0
    values = jax.random.normal(rng, shape, jnp.float32) * deviation * level
    return jnp.minimum(jnp.maximum(values, -bound), bound).astype(held_as)


def setup_inputs(seed: int = 0) -> dict:
    streams_of = jax.random.split(jax.random.key(seed), 6)
    return {
        "query": draw_query(jax.random.fold_in(streams_of[5], 71), 0),
        "key": draw_key(jax.random.fold_in(streams_of[5], 71), 0),
        "value": noise(streams_of[2], (SAMPLES, TOKENS, WIDTH), 2.0, 12.0, ((0, 8), (1, 64))),
        "gains": draw_gains(jax.random.fold_in(streams_of[5], 71), 0),
        "d_mixed": noise(streams_of[4], (SAMPLES, SPLIT, ROWS, FRAMES, WIDTH), 2.0, 12.0, ((0, 8), (2, 64))),
    }


def normalize(values):
    widened = values.astype(jnp.float32)
    factor = lax.rsqrt(lax.optimization_barrier(jnp.mean(widened * widened, axis=-1, keepdims=True)) + 1e-06)
    return (widened * factor, factor)

def norm_back(x_hat, factor, gain, incoming):
    scaled = incoming * gain
    return factor * (scaled - x_hat * lax.optimization_barrier(jnp.mean(scaled * x_hat, axis=-1, keepdims=True)))

def attend(queries, keys, values):
    factor = queries.shape[-1] ** (-0.5)

    def one_head(items):
        heads_q, heads_k, heads_v = items
        scores = jnp.einsum('nqd,nkd->nqk', heads_q.astype(jnp.float32), heads_k.astype(jnp.float32)) * factor
        peak = lax.optimization_barrier(jnp.max(scores, axis=-1, keepdims=True))
        total = peak + jnp.log(lax.optimization_barrier(jnp.sum(jnp.exp(scores - peak), axis=-1, keepdims=True)))
        weights = jnp.exp(scores - total).astype(jnp.bfloat16)
        result = jnp.einsum('nqk,nkd->nqd', weights.astype(jnp.float32), heads_v.astype(jnp.float32))
        return (result.astype(jnp.bfloat16), total)
    result, total = lax.map(one_head, (jnp.moveaxis(queries, 2, 0), jnp.moveaxis(keys, 2, 0), jnp.moveaxis(values, 2, 0)))
    return (jnp.moveaxis(result, 0, 2), total)

def attend_back(queries, keys, values, d_out, result, total):
    factor = queries.shape[-1] ** (-0.5)

    def one_head(items):
        heads_q, heads_k, heads_v, heads_d, heads_o, head_total = items
        scores = jnp.einsum('nqd,nkd->nqk', heads_q.astype(jnp.float32), heads_k.astype(jnp.float32)) * factor
        weights = jnp.exp(scores - head_total)
        rounded = weights.astype(jnp.bfloat16)
        d_weights = jnp.einsum('nqd,nkd->nqk', heads_d.astype(jnp.float32), heads_v.astype(jnp.float32))
        delta = lax.optimization_barrier(jnp.sum(heads_d.astype(jnp.float32) * heads_o.astype(jnp.float32), axis=-1, keepdims=True))
        d_scores = (weights * (d_weights - delta) * factor).astype(jnp.bfloat16)
        d_query = jnp.einsum('nqk,nkd->nqd', d_scores.astype(jnp.float32), heads_k.astype(jnp.float32))
        d_key = jnp.einsum('nqk,nqd->nkd', d_scores.astype(jnp.float32), heads_q.astype(jnp.float32))
        d_value = jnp.einsum('nqk,nqd->nkd', rounded.astype(jnp.float32), heads_d.astype(jnp.float32))
        return (d_query, d_key, d_value)
    d_query, d_key, d_value = lax.map(one_head, (jnp.moveaxis(queries, 2, 0), jnp.moveaxis(keys, 2, 0), jnp.moveaxis(values, 2, 0), jnp.moveaxis(d_out, 2, 0), jnp.moveaxis(result, 2, 0), total))
    return (jnp.moveaxis(d_query, 0, 2), jnp.moveaxis(d_key, 0, 2), jnp.moveaxis(d_value, 0, 2))

def one_sample(query, key, value, d_mixed, gains):
    heads = query.shape[-1] // HD
    shape = (FRAMES, PATCHES, heads, HD)
    order = (1, 0, 2, 3)
    q_hat, q_factor = normalize(query.reshape(shape))
    k_hat, k_factor = normalize(key.reshape(shape))
    values = value.reshape(shape)
    q_space = (q_hat * gains[0]).astype(jnp.bfloat16)
    k_space = (k_hat * gains[1]).astype(jnp.bfloat16)
    o_space, total_space = attend(q_space, k_space, values)
    tq_hat = q_hat.transpose(order)
    tq_factor = q_factor.transpose(order)
    tk_hat = k_hat.transpose(order)
    tk_factor = k_factor.transpose(order)
    q_time = (tq_hat * gains[2]).astype(jnp.bfloat16)
    k_time = (tk_hat * gains[3]).astype(jnp.bfloat16)
    time_values = o_space.transpose(order)
    mixed, total_time = attend(q_time, k_time, time_values)
    d_time = d_mixed.reshape(PATCHES, FRAMES, heads, HD)
    dqn_time, dkn_time, d_values = attend_back(q_time, k_time, time_values, d_time, mixed, total_time)
    d_space = d_values.astype(jnp.bfloat16).transpose(order)
    dq_time = norm_back(tq_hat, tq_factor, gains[2], dqn_time).astype(jnp.bfloat16).transpose(order)
    dk_time = norm_back(tk_hat, tk_factor, gains[3], dkn_time).astype(jnp.bfloat16).transpose(order)
    dqn_space, dkn_space, dv_space = attend_back(q_space, k_space, values, d_space, o_space, total_space)
    query_grad = (norm_back(q_hat, q_factor, gains[0], dqn_space) + dq_time.astype(jnp.float32)).astype(jnp.bfloat16)
    key_grad = (norm_back(k_hat, k_factor, gains[1], dkn_space) + dk_time.astype(jnp.float32)).astype(jnp.bfloat16)
    value_grad = dv_space.astype(jnp.bfloat16)
    sums = jnp.stack([lax.optimization_barrier(jnp.sum(dqn_space * q_hat, axis=(0, 1, 2))), lax.optimization_barrier(jnp.sum(dkn_space * k_hat, axis=(0, 1, 2))), lax.optimization_barrier(jnp.sum(dqn_time * tq_hat, axis=(0, 1, 2))), lax.optimization_barrier(jnp.sum(dkn_time * tk_hat, axis=(0, 1, 2)))])
    width = heads * HD
    return (mixed.reshape(SPLIT, ROWS, FRAMES, width), query_grad.reshape(TOKENS, width), key_grad.reshape(TOKENS, width), value_grad.reshape(TOKENS, width), sums)

def reference(query, key, value, gains, d_mixed):

    def sample_step(items):
        return one_sample(items[0], items[1], items[2], items[3], gains)
    mixed, query_grad, key_grad, value_grad, sums = lax.map(sample_step, (query, key, value, d_mixed))
    return (mixed, query_grad, key_grad, value_grad, lax.optimization_barrier(jnp.sum(sums, axis=0)))
```

```python
import jax
import jax.numpy as jnp
from jax import lax
from jax.experimental import pallas as pl
from jax.experimental.pallas import tpu as pltpu
from jax.sharding import PartitionSpec as P

SEQ = 64
DP = 8
WIDTH = 2048
HALF = 1024
PART = 512
HD = 128
ROWS = 128
FRAMES = 32
EPS = 1e-06
SCALE = HD**-0.5
SCALE2 = SCALE * 1.4426950408889634
BF = jnp.bfloat16
F32 = jnp.float32


def dot(a, b, dims):
    return lax.dot_general(a, b, (dims, ((), ())), preferred_element_type=F32)


NN = ((1,), (0,))
NT = ((1,), (1,))
TN = ((0,), (0,))


def selector(column_of_row):
    row = lax.broadcasted_iota(jnp.int32, (256, 256), 0)
    column = lax.broadcasted_iota(jnp.int32, (256, 256), 1)
    return jnp.where(column == column_of_row(row), 1.0, 0.0).astype(BF)


def space_to_chunk(o):
    return (o & 3) * 64 + ((o >> 2) & 1) * 32 + (o >> 4) * 2 + ((o >> 3) & 1)


def chunk_to_space(i):
    return ((i & 31) >> 1) * 16 + (i & 1) * 8 + ((i >> 5) & 1) * 4 + (i >> 6)


def chunk_to_time(o):
    return (o & 15) * 16 + ((o >> 4) & 1) * 8 + ((o >> 5) & 1) * 4 + (o >> 6)


def time_to_chunk(i):
    return (i & 3) * 64 + (((i >> 2) & 1) * 2 + ((i >> 3) & 1)) * 16 + (i >> 4)


def hat(values):
    factor = lax.rsqrt(jnp.sum(values * values, axis=-1, keepdims=True) * (1.0 / HD) + EPS)
    return values * factor, factor


def softmax(scores):
    peak = jnp.max(scores, axis=-1, keepdims=True)
    raised = jnp.exp2((scores - peak) * SCALE2)
    return raised * (1.0 / jnp.sum(raised, axis=-1, keepdims=True))


def norm_back(x_hat, factor, gain, incoming):
    product = incoming * x_hat
    mean = jnp.sum(product * gain, axis=-1, keepdims=True) * (1.0 / HD)
    return factor * (incoming * gain - x_hat * mean), product


def fold(product):
    return jnp.sum(product.reshape(-1, 8, HD), axis=0)


def kernel(
    query, key, value, gains, d_mixed,
    mixed, query_grad, key_grad, value_grad, gain_grads,
    select, frame, d_time, probs, o_space, send_qk, send_o, got_qk, got_o,
    time_in, time_out, time_mixed, send_d, send_dqk, got_d, got_dqk, d_space, back, final,
    sums, gathered,
    own_sem, trade_send, trade_recv, mixed_in_sem, mixed_sem,
    qk_send, qk_recv, o_send, o_recv, d_send, d_recv, dqk_send, dqk_recv,
    out_sem, out_send, out_recv, sum_send, sum_recv,
):
    me = lax.axis_index("seq")
    sample = lax.axis_index("dp")
    z, x, y = me // 32, (me // 8) % 4, me % 8
    half, frame_at = me % 2, me // 2
    partner = me + 1 - 2 * half

    def peer(step):
        return (
            ((z + step // 32) % 2) * 32 + ((x + (step // 8) % 4) % 4) * 8 + (y + step % 8) % 8
        )

    def frame_peer(step):
        return (
            ((z + step // 16) % 2) * 16
            + ((x + (step // 4) % 4) % 4) * 4
            + (y // 2 + step % 4) % 4
        )

    inputs = (query, key, value)
    outputs = (query_grad, key_grad, value_grad)

    def own_copy(a, g):
        return pltpu.make_async_copy(
            inputs[a].at[:, pl.ds(half * HALF + g * PART, PART)],
            frame.at[a, half, :, pl.ds(g * PART, PART)],
            own_sem.at[a, g],
        )

    def trade_copy(a, g):
        return pltpu.make_async_remote_copy(
            src_ref=inputs[a].at[:, pl.ds((1 - half) * HALF + g * PART, PART)],
            dst_ref=frame.at[a, half, :, pl.ds(g * PART, PART)],
            send_sem=trade_send.at[a, g],
            recv_sem=trade_recv.at[a, g],
            device_id={"seq": partner},
            device_id_type=pl.DeviceIdType.MESH,
        )

    for g in range(2):
        for a in range(3):
            own_copy(a, g).start()
    mixed_in = pltpu.make_async_copy(d_mixed, d_time, mixed_in_sem)
    mixed_in.start()

    barrier = pltpu.get_barrier_semaphore()

    @pl.loop(1, SEQ)
    def _(step):
        pl.semaphore_signal(
            barrier, inc=1, device_id={"seq": peer(step)}, device_id_type=pl.DeviceIdType.MESH
        )

    @pl.loop(1, DP)
    def _(step):
        pl.semaphore_signal(
            barrier,
            inc=1,
            device_id={"dp": (sample + step) % DP},
            device_id_type=pl.DeviceIdType.MESH,
        )

    for i, source in enumerate((space_to_chunk, chunk_to_space, chunk_to_time, time_to_chunk)):
        select[i] = selector(source)
    sums[...] = jnp.zeros_like(sums)

    pl.semaphore_wait(barrier, SEQ - 1 + DP - 1)

    for g in range(2):
        for a in range(3):
            trade_copy(a, g).start()

    gain = [gains[i : i + 1, :] for i in range(4)]

    def send_all(source, target, send_sem, recv_sem):
        pltpu.make_async_copy(source.at[me], target.at[frame_at], recv_sem).start()

        @pl.loop(1, SEQ)
        def _(step):
            to = peer(step)
            pltpu.make_async_remote_copy(
                src_ref=source.at[to],
                dst_ref=target.at[frame_at],
                send_sem=send_sem,
                recv_sem=recv_sem,
                device_id={"seq": to},
                device_id_type=pl.DeviceIdType.MESH,
            ).start()

    def wait_bytes(ref, sem):
        pltpu.make_async_copy(ref, ref, sem).wait()

    @pl.loop(0, 2)
    def _(g):
        for a in range(2):
            own_copy(a, g).wait()
            trade_copy(a, g).wait_recv()

        @pl.loop(0, 4)
        def _(b):
            pieces = []
            for a in range(2):
                pieces.append(
                    jnp.concatenate(
                        [
                            frame[a, r, pl.ds(b * 32, 32), pl.ds(g * PART + h * HD, HD)]
                            for h in range(4)
                            for r in range(2)
                        ],
                        axis=0,
                    )
                )
            moved = dot(select[0], jnp.concatenate(pieces, axis=1), NN).astype(BF)
            for a in range(2):
                send_qk[g, pl.ds(b * 16, 16), a] = moved[:, a * HD : (a + 1) * HD].reshape(16, 16, HD)

        slot = g * 2 + half
        send_all(send_qk.at[g], got_qk.at[slot], qk_send.at[g], qk_recv.at[slot])
        own_copy(2, g).wait()
        trade_copy(2, g).wait_recv()

        @pl.loop(0, 4)
        def _(h):
            columns = pl.ds(pl.multiple_of(g * PART + h * HD, HD), HD)
            q_hat, _ = hat(frame[0, :, :, columns].reshape(256, HD).astype(F32))
            k_hat, _ = hat(frame[1, :, :, columns].reshape(256, HD).astype(F32))
            q = (q_hat * gain[0]).astype(BF)
            k = (k_hat * gain[1]).astype(BF)
            weights = softmax(dot(q, k, NT))
            probs[g * 4 + h] = weights
            result = dot(weights.astype(BF), frame[2, :, :, columns].reshape(256, HD), NN)
            o_space[g, h] = result.astype(BF).reshape(2, 4, 32, HD)

        @pl.loop(0, 4)
        def _(b):
            moved = dot(select[0], o_space[g, :, :, b].reshape(256, HD), NN).astype(BF)
            send_o[g, pl.ds(b * 16, 16)] = moved.reshape(16, 16, HD)

        send_all(send_o.at[g], got_o.at[slot], o_send.at[g], o_recv.at[slot])

    mixed_in.wait()
    group = lax.broadcasted_iota(jnp.int32, (ROWS, ROWS), 0) // FRAMES
    same = group == lax.broadcasted_iota(jnp.int32, (ROWS, ROWS), 1) // FRAMES

    @pl.loop(0, 4)
    def _(t):
        to_half = t % 2
        g = t // 2
        wait_bytes(got_qk.at[t], qk_recv.at[t])
        wait_bytes(got_o.at[t], o_recv.at[t])
        for part in range(2):
            here = pl.ds(part * 16, 16)
            blocks = [got_qk[t, here, 0], got_qk[t, here, 1], got_o[t, here]]
            moved = dot(
                select[2], jnp.concatenate([b.reshape(256, HD) for b in blocks], axis=1), NN
            )
            for a in range(3):
                time_in[a, :, :, part] = moved[:, a * HD : (a + 1) * HD].reshape(4, 4, 16, HD)

        @pl.loop(0, 4)
        def _(h):
            columns = pl.ds(pl.multiple_of(to_half * HALF + g * PART + h * HD, HD), HD)
            q_hat, q_factor = hat(time_in[0, h].reshape(ROWS, HD))
            k_hat, k_factor = hat(time_in[1, h].reshape(ROWS, HD))
            o = time_in[2, h].reshape(ROWS, HD).astype(BF)
            q = (q_hat * gain[2]).astype(BF)
            k = (k_hat * gain[3]).astype(BF)
            weights = softmax(jnp.where(same, dot(q, k, NT), -1e30))
            rounded = weights.astype(BF)
            result = dot(rounded, o, NN).astype(BF)
            time_mixed[:, columns] = result
            d_out = d_time[:, columns]
            delta = jnp.sum(d_out.astype(F32) * result.astype(F32), axis=-1, keepdims=True)
            d_scores = (weights * (dot(d_out, o, NT) - delta) * SCALE).astype(BF)
            d_q, product = norm_back(q_hat, q_factor, gain[2], dot(d_scores, k, NN))
            sums[2] += fold(product)
            d_k, product = norm_back(k_hat, k_factor, gain[3], dot(d_scores, q, TN))
            sums[3] += fold(product)
            d_o = dot(rounded, d_out, TN)
            for a, one in enumerate((d_o, d_q, d_k)):
                time_out[a, h] = one.astype(BF).reshape(4, 2, 16, HD)

        for part in range(2):
            moved = dot(
                select[3],
                jnp.concatenate([time_out[a, :, :, part].reshape(256, HD) for a in range(3)], axis=1),
                NN,
            ).astype(BF)
            here = pl.ds(part * 16, 16)
            send_d[t, here] = moved[:, :HD].reshape(16, 16, HD)
            send_dqk[t, here, 0] = moved[:, HD : 2 * HD].reshape(16, 16, HD)
            send_dqk[t, here, 1] = moved[:, 2 * HD :].reshape(16, 16, HD)

        def send_back(source, target, send_sem, recv_sem):
            def one(step):
                to = frame_peer(step)
                pltpu.make_async_remote_copy(
                    src_ref=source.at[to],
                    dst_ref=target.at[me],
                    send_sem=send_sem,
                    recv_sem=recv_sem,
                    device_id={"seq": to * 2 + to_half},
                    device_id_type=pl.DeviceIdType.MESH,
                ).start()

            @pl.when(to_half == half)
            def _():
                pltpu.make_async_copy(source.at[frame_at], target.at[me], recv_sem).start()

            @pl.when(to_half != half)
            def _():
                one(0)

            pl.loop(1, FRAMES)(one)

        send_back(send_d.at[t], got_d.at[g], d_send, d_recv.at[g])
        send_back(send_dqk.at[t], got_dqk.at[g], dqk_send, dqk_recv.at[g])

    mixed_out = pltpu.make_async_copy(time_mixed, mixed, mixed_sem)
    mixed_out.start()

    def out_own(a, g):
        return pltpu.make_async_copy(
            final.at[a, half, :, pl.ds(g * PART, PART)],
            outputs[a].at[:, pl.ds(half * HALF + g * PART, PART)],
            out_sem.at[a, g],
        )

    def out_trade(a, g):
        return pltpu.make_async_remote_copy(
            src_ref=final.at[a, 1 - half, :, pl.ds(g * PART, PART)],
            dst_ref=outputs[a].at[:, pl.ds(half * HALF + g * PART, PART)],
            send_sem=out_send.at[a, g],
            recv_sem=out_recv.at[a, g],
            device_id={"seq": partner},
            device_id_type=pl.DeviceIdType.MESH,
        )

    @pl.loop(0, 2)
    def _(g):
        wait_bytes(got_d.at[g], d_recv.at[g])

        @pl.loop(0, 4)
        def _(b):
            moved = dot(select[1], got_d[g, pl.ds(b * 16, 16)].reshape(256, HD), NN).astype(BF)
            d_space[:, :, b] = moved.reshape(4, 2, 32, HD)

        @pl.loop(0, 4)
        def _(h):
            columns = pl.ds(pl.multiple_of(g * PART + h * HD, HD), HD)
            q_hat, q_factor = hat(frame[0, :, :, columns].reshape(256, HD).astype(F32))
            k_hat, k_factor = hat(frame[1, :, :, columns].reshape(256, HD).astype(F32))
            q = (q_hat * gain[0]).astype(BF)
            k = (k_hat * gain[1]).astype(BF)
            v = frame[2, :, :, columns].reshape(256, HD)
            weights = probs[g * 4 + h]
            d_out = d_space[h].reshape(256, HD)
            result = o_space[g, h].reshape(256, HD)
            delta = jnp.sum(d_out.astype(F32) * result.astype(F32), axis=-1, keepdims=True)
            d_scores = (weights * (dot(d_out, v, NT) - delta) * SCALE).astype(BF)
            d_q, product = norm_back(q_hat, q_factor, gain[0], dot(d_scores, k, NN))
            sums[0] += fold(product)
            back[0, h] = d_q.reshape(2, 4, 32, HD)
            d_k, product = norm_back(k_hat, k_factor, gain[1], dot(d_scores, q, TN))
            sums[1] += fold(product)
            back[1, h] = d_k.reshape(2, 4, 32, HD)
            d_v = dot(weights.astype(BF), d_out, TN)
            final[2, :, :, columns] = d_v.astype(BF).reshape(2, ROWS, HD)

        wait_bytes(got_dqk.at[g], dqk_recv.at[g])

        @pl.loop(0, 4)
        def _(b):
            here = pl.ds(b * 16, 16)
            moved = dot(
                select[1],
                jnp.concatenate([got_dqk[g, here, a].reshape(256, HD) for a in range(2)], axis=1),
                NN,
            )
            for a in range(2):
                for h in range(4):
                    for r in range(2):
                        at = h * 64 + r * 32
                        total = moved[at : at + 32, a * HD : (a + 1) * HD] + back[a, h, r, b]
                        columns = pl.ds(pl.multiple_of(g * PART + h * HD, HD), HD)
                        final[a, r, pl.ds(b * 32, 32), columns] = total.astype(BF)

        for a in range(3):
            out_trade(a, g).start()
            out_own(a, g).start()

    own = jnp.sum(sums[...], axis=1)
    total = jnp.concatenate([own, jnp.zeros_like(own)], axis=0)
    rounds = (
        (z * 4 + x, lambda at: {"seq": at * 8 + y}),
        (y, lambda at: {"seq": z * 32 + x * 8 + at}),
        (sample, lambda at: {"dp": at}),
    )
    for i, (place, device) in enumerate(rounds):
        gathered[i, place] = total

        @pl.loop(1, 8)
        def _(step):
            pltpu.make_async_remote_copy(
                src_ref=gathered.at[i, place],
                dst_ref=gathered.at[i, place],
                send_sem=sum_send.at[i],
                recv_sem=sum_recv.at[i],
                device_id=device((place + step) % 8),
                device_id_type=pl.DeviceIdType.MESH,
            ).start()

        wait_bytes(gathered.at[i, pl.ds(0, 7)], sum_recv.at[i])
        total = jnp.sum(gathered[i], axis=0)
    gain_grads[...] = total[0:4]

    for i in range(3):
        wait_bytes(gathered.at[i, pl.ds(0, 7)], sum_send.at[i])
    for g in range(2):
        for a in range(3):
            trade_copy(a, g).wait_send()
            out_trade(a, g).wait()
            out_own(a, g).wait()
        wait_bytes(send_qk.at[g, pl.ds(0, SEQ - 1)], qk_send.at[g])
        wait_bytes(send_o.at[g, pl.ds(0, SEQ - 1)], o_send.at[g])
    wait_bytes(got_d.at[:, pl.ds(0, SEQ - 1)], d_send)
    wait_bytes(got_dqk.at[:, pl.ds(0, SEQ - 1)], dqk_send)
    mixed_out.wait()


def body(query, key, value, gains, d_mixed):
    wide = (ROWS, WIDTH)
    any_spec = pl.BlockSpec(memory_space=pl.ANY)
    vmem_spec = pl.BlockSpec(memory_space=pltpu.VMEM)
    dma = pltpu.SemaphoreType.DMA
    mixed, query_grad, key_grad, value_grad, gain_grads = pl.pallas_call(
        kernel,
        out_shape=[jax.ShapeDtypeStruct(wide, BF)] * 4 + [jax.ShapeDtypeStruct((4, HD), F32)],
        in_specs=[any_spec, any_spec, any_spec, vmem_spec, any_spec],
        out_specs=[any_spec, any_spec, any_spec, any_spec, vmem_spec],
        scratch_shapes=[
            pltpu.VMEM((4, 256, 256), BF),
            pltpu.VMEM((3, 2, ROWS, HALF), BF),
            pltpu.VMEM(wide, BF),
            pltpu.VMEM((8, 256, 256), F32),
            pltpu.VMEM((2, 4, 2, 4, 32, HD), BF),
            pltpu.VMEM((2, SEQ, 2, 16, HD), BF),
            pltpu.VMEM((2, SEQ, 16, HD), BF),
            pltpu.VMEM((4, FRAMES, 2, 16, HD), BF),
            pltpu.VMEM((4, FRAMES, 16, HD), BF),
            pltpu.VMEM((3, 4, 4, 2, 16, HD), F32),
            pltpu.VMEM((3, 4, 4, 2, 16, HD), BF),
            pltpu.VMEM(wide, BF),
            pltpu.VMEM((4, FRAMES, 16, HD), BF),
            pltpu.VMEM((4, FRAMES, 2, 16, HD), BF),
            pltpu.VMEM((2, SEQ, 16, HD), BF),
            pltpu.VMEM((2, SEQ, 2, 16, HD), BF),
            pltpu.VMEM((4, 2, 4, 32, HD), BF),
            pltpu.VMEM((2, 4, 2, 4, 32, HD), F32),
            pltpu.VMEM((3, 2, ROWS, HALF), BF),
            pltpu.VMEM((4, 8, HD), F32),
            pltpu.VMEM((3, 8, 8, HD), F32),
            dma((3, 2)),
            dma((3, 2)),
            dma((3, 2)),
            dma,
            dma,
            dma((2,)),
            dma((4,)),
            dma((2,)),
            dma((4,)),
            dma,
            dma((2,)),
            dma,
            dma((2,)),
            dma((3, 2)),
            dma((3, 2)),
            dma((3, 2)),
            dma((3,)),
            dma((3,)),
        ],
        compiler_params=pltpu.CompilerParams(
            collective_id=0, has_side_effects=True, vmem_limit_bytes=40 * 2**20
        ),
        cost_estimate=pl.CostEstimate(flops=2 * 10**9, bytes_accessed=2**22, transcendentals=10**6),
        name="space_time_attention",
    )(query.reshape(wide), key.reshape(wide), value.reshape(wide), gains, d_mixed.reshape(wide))
    return (
        mixed.reshape(d_mixed.shape),
        query_grad.reshape(query.shape),
        key_grad.reshape(key.shape),
        value_grad.reshape(value.shape),
        gain_grads,
    )


def solution(mesh):
    placed = (
        P("dp", "seq", None),
        P("dp", "seq", None),
        P("dp", "seq", None),
        P(),
        P("dp", None, "seq", None, None),
    )
    return jax.shard_map(
        body,
        mesh=mesh,
        in_specs=placed,
        out_specs=(
            P("dp", None, "seq", None, None),
            P("dp", "seq", None),
            P("dp", "seq", None),
            P("dp", "seq", None),
            P(),
        ),
        check_vma=False,
    )
```

```python
import jax
import jax.numpy as jnp
from jax import lax
from jax.experimental import pallas as pl
from jax.experimental.pallas import tpu as pltpu
from jax.sharding import PartitionSpec as P

SEQ = 64
DP = 8
WIDTH = 2048
HALF = 1024
PART = 512
HD = 128
ROWS = 128
FRAMES = 32
EPS = 1e-06
SCALE = HD**-0.5
SCALE2 = SCALE * 1.4426950408889634
BF = jnp.bfloat16
F32 = jnp.float32


def dot(a, b, dims):
    return lax.dot_general(a, b, (dims, ((), ())), preferred_element_type=F32)


NN = ((1,), (0,))
NT = ((1,), (1,))
TN = ((0,), (0,))


def selector(column_of_row):
    row = lax.broadcasted_iota(jnp.int32, (256, 256), 0)
    column = lax.broadcasted_iota(jnp.int32, (256, 256), 1)
    return jnp.where(column == column_of_row(row), 1.0, 0.0).astype(BF)


def from_space(o):
    return (o & 3) * 64 + ((o >> 2) & 1) * 32 + (o >> 4) * 2 + ((o >> 3) & 1)


def to_space(i):
    return ((i & 31) >> 1) * 16 + (i & 1) * 8 + ((i >> 5) & 1) * 4 + (i >> 6)


def to_time(o):
    return (o & 15) * 16 + ((o >> 4) & 1) * 8 + ((o >> 5) & 1) * 4 + (o >> 6)


def from_time(i):
    return (i & 3) * 64 + (((i >> 2) & 1) * 2 + ((i >> 3) & 1)) * 16 + (i >> 4)


def from_rows(o):
    return (o & 7) * 32 + (o >> 4) * 2 + ((o >> 3) & 1)


def to_rows(i):
    return ((i & 31) >> 1) * 16 + (i & 1) * 8 + (i >> 5)


def to_time8(o):
    return (o & 7) * 32 + ((o >> 4) & 1) * 16 + ((o >> 3) & 1) * 8 + (o >> 5)


def from_time8(c):
    return (c & 7) * 32 + (((c >> 4) & 1) * 2 + ((c >> 3) & 1)) * 8 + (c >> 5)


SELECTORS = (from_space, to_space, to_time, from_time, from_rows, to_rows, to_time8, from_time8)


def hat(values):
    factor = lax.rsqrt(jnp.sum(values * values, axis=-1, keepdims=True) * (1.0 / HD) + EPS)
    return values * factor, factor


def softmax(scores):
    peak = jnp.max(scores, axis=-1, keepdims=True)
    raised = jnp.exp2((scores - peak) * SCALE2)
    return raised * (1.0 / jnp.sum(raised, axis=-1, keepdims=True))


def norm_back(x_hat, factor, gain, incoming):
    product = incoming * x_hat
    mean = jnp.sum(product * gain, axis=-1, keepdims=True) * (1.0 / HD)
    return factor * (incoming * gain - x_hat * mean), product


def fold(product):
    return jnp.sum(product.reshape(-1, 8, HD), axis=0)


def kernel(
    query, key, value, gains_in, d_mixed,
    mixed, query_grad, key_grad, value_grad, gain_grads,
    gains, select, native, frame, d_time, probs, o_space, send_native, send_relay, send_o, got_qk, got_o,
    time_qk, time_o, time_d, time_dqk, time_mixed, send_d, send_dqk, got_d, got_own, got_head,
    got_token, d_space, back, final_out, final_own, final_in, final_sum, sums, gathered,
    gains_sem, native_sem, own_sem, trade_send, trade_recv, mixed_in_sem, mixed_sem,
    native_send, relay_send, qk_recv, o_send, o_recv, d_send, d_recv,
    head_send, token_send, back_send, head_recv, token_recv, back_recv,
    out_sem, out_send, out_recv, sum_sem, sum_send, sum_recv,
):
    me = lax.axis_index("seq")
    sample = lax.axis_index("dp")
    z, x, y = me // 32, (me // 8) % 4, me % 8
    half, frame_at = me % 2, me // 2
    other = 1 - half
    partner = me + 1 - 2 * half

    def device_at(step, dy):
        return ((z + step // 16) % 2) * 32 + ((x + (step // 4) % 4) % 4) * 8 + (y + 8 + dy) % 8

    def peer(step):
        return (
            ((z + step // 32) % 2) * 32 + ((x + (step // 8) % 4) % 4) * 8 + (y + step % 8) % 8
        )

    def near_peer(step):
        return device_at(step, (step % 4) * (2 * half - 1))

    def far_peer(step):
        return device_at(step, (step % 4 + 1) * (1 - 2 * half))

    def frame_peer(step):
        return (
            ((z + step // 16) % 2) * 16
            + ((x + (step // 4) % 4) % 4) * 4
            + (y // 2 + step % 4) % 4
        )

    def remote(source, target, send_sem, recv_sem, to):
        return pltpu.make_async_remote_copy(
            src_ref=source,
            dst_ref=target,
            send_sem=send_sem,
            recv_sem=recv_sem,
            device_id=to if isinstance(to, dict) else {"seq": to},
            device_id_type=pl.DeviceIdType.MESH,
        )

    def wait_bytes(ref, sem):
        pltpu.make_async_copy(ref, ref, sem).wait()

    inputs = (query, key, value)
    outputs = (query_grad, key_grad, value_grad)

    def own_copy(a, g):
        return pltpu.make_async_copy(
            inputs[a].at[:, pl.ds(half * HALF + g * PART, PART)],
            frame.at[a, half, :, pl.ds(g * PART, PART)],
            own_sem.at[a, g],
        )

    def trade_copy(a, g):
        return remote(
            inputs[a].at[:, pl.ds(other * HALF + g * PART, PART)],
            frame.at[a, half, :, pl.ds(g * PART, PART)],
            trade_send.at[a, g],
            trade_recv.at[a, g],
            partner,
        )

    gains_copy = pltpu.make_async_copy(gains_in, gains, gains_sem)
    gains_copy.start()
    native_copies = [
        pltpu.make_async_copy(inputs[a], native.at[a], native_sem.at[a]) for a in range(2)
    ]
    for copy in native_copies:
        copy.start()
    for g in range(2):
        for a in range(3):
            own_copy(a, g).start()
    mixed_in = pltpu.make_async_copy(d_mixed, d_time, mixed_in_sem)
    mixed_in.start()
    got_head[...] = jnp.zeros_like(got_head)
    got_token[...] = jnp.zeros_like(got_token)

    barrier = pltpu.get_barrier_semaphore()

    @pl.loop(1, SEQ)
    def _(step):
        pl.semaphore_signal(
            barrier, inc=1, device_id={"seq": peer(step)}, device_id_type=pl.DeviceIdType.MESH
        )

    @pl.loop(1, DP)
    def _(step):
        pl.semaphore_signal(
            barrier,
            inc=1,
            device_id={"dp": (sample + step) % DP},
            device_id_type=pl.DeviceIdType.MESH,
        )

    pl.semaphore_wait(barrier, SEQ - 1 + DP - 1)

    for g in range(2):
        for a in range(3):
            trade_copy(a, g).start()

    for i, source in enumerate(SELECTORS):
        select[i] = selector(source)
    sums[...] = jnp.zeros_like(sums)
    gains_copy.wait()
    gain = [gains[i : i + 1, :] for i in range(4)]

    def rows_to_units(source, block, first, target):
        pieces = [
            jnp.concatenate(
                [source(a)[pl.ds(block * 32, 32), pl.ds(first + h * HD, HD)] for h in range(8)], axis=0
            )
            for a in range(2)
        ]
        moved = dot(select[4], jnp.concatenate(pieces, axis=1), NN).astype(BF)
        for a in range(2):
            target(pl.ds(block * 16, 16), a, moved[:, a * HD : (a + 1) * HD].reshape(16, 16, HD))

    for copy in native_copies:
        copy.wait()

    for hh in range(2):

        def put(devices, a, units):
            send_native[devices, hh, a] = units

        for block in range(4):
            rows_to_units(lambda a: native.at[a], block, hh * HALF, put)

    @pl.loop(0, 2)
    def _(g):
        for a in range(3):
            own_copy(a, g).wait()
            trade_copy(a, g).wait_recv()

        @pl.when(g == 0)
        def _():
            pltpu.make_async_copy(send_native.at[me], got_qk.at[frame_at, half], qk_recv).start()

            @pl.loop(1, 32)
            def _(step):
                to = near_peer(step)
                remote(send_native.at[to], got_qk.at[frame_at, half], native_send, qk_recv, to).start()

            @pl.loop(0, 32)
            def _(step):
                to = far_peer(step)
                remote(
                    send_native.at[to, half], got_qk.at[frame_at, half, half], native_send, qk_recv, to
                ).start()

        @pl.loop(0, 4)
        def _(h):
            columns = pl.ds(pl.multiple_of(g * PART + h * HD, HD), HD)
            q_hat, _ = hat(frame[0, :, :, columns].reshape(256, HD).astype(F32))
            k_hat, _ = hat(frame[1, :, :, columns].reshape(256, HD).astype(F32))
            q = (q_hat * gain[0]).astype(BF)
            k = (k_hat * gain[1]).astype(BF)
            weights = softmax(dot(q, k, NT))
            probs[g * 4 + h] = weights
            result = dot(weights.astype(BF), frame[2, :, :, columns].reshape(256, HD), NN)
            o_space[g, h] = result.astype(BF).reshape(2, 4, 32, HD)

        for b in range(4):
            moved = dot(select[0], o_space[g, :, :, b].reshape(256, HD), NN).astype(BF)
            send_o[g, pl.ds(b * 16, 16)] = moved.reshape(16, 16, HD)

        slot = g * 2 + half
        pltpu.make_async_copy(send_o.at[g, me], got_o.at[slot, frame_at], o_recv.at[slot]).start()

        @pl.loop(1, SEQ)
        def _(step):
            to = peer(step)
            remote(
                send_o.at[g, to], got_o.at[slot, frame_at], o_send.at[g], o_recv.at[slot], to
            ).start()

    def put_relay(devices, a, units):
        send_relay[devices, a] = units

    for block in range(4):
        rows_to_units(lambda a: frame.at[a, other], block, 0, put_relay)

    pltpu.make_async_copy(send_relay.at[me], got_qk.at[frame_at, other, half], qk_recv).start()

    @pl.loop(1, 32)
    def _(step):
        to = near_peer(step)
        remote(
            send_relay.at[to], got_qk.at[frame_at, other, half], relay_send, qk_recv, to
        ).start()

    wait_bytes(got_qk, qk_recv)
    for hh in range(2):
        for part in range(4):
            here = pl.ds(part * 8, 8)
            units = [got_qk[here, :, hh, a].reshape(256, HD) for a in range(2)]
            moved = dot(select[6], jnp.concatenate(units, axis=1), NN)
            for a in range(2):
                time_qk[hh, a, :, :, part] = moved[:, a * HD : (a + 1) * HD].reshape(8, 4, 8, HD)

    mixed_in.wait()
    group = lax.broadcasted_iota(jnp.int32, (ROWS, ROWS), 0) // FRAMES
    same = group == lax.broadcasted_iota(jnp.int32, (ROWS, ROWS), 1) // FRAMES

    @pl.loop(0, 4)
    def _(t):
        hh = t % 2
        g = t // 2
        wait_bytes(got_o.at[t], o_recv.at[t])
        for part in range(2):
            units = got_o[t, pl.ds(part * 16, 16)].reshape(256, HD)
            time_o[:, :, part] = dot(select[2], units, NN).astype(BF).reshape(4, 4, 16, HD)

        heads = range(4)

        def each(one, *stacked):
            return jnp.concatenate(
                [one(*(values[h * ROWS : (h + 1) * ROWS] for values in stacked)) for h in heads], axis=0
            )

        columns = [
            pl.ds(pl.multiple_of(hh * HALF + g * PART + h * HD, HD), HD) for h in heads
        ]
        q_hat, q_factor = hat(time_qk[hh, 0, pl.ds(g * 4, 4)].reshape(4 * ROWS, HD))
        k_hat, k_factor = hat(time_qk[hh, 1, pl.ds(g * 4, 4)].reshape(4 * ROWS, HD))
        o = time_o[...].reshape(4 * ROWS, HD)
        q = (q_hat * gain[2]).astype(BF)
        k = (k_hat * gain[3]).astype(BF)
        scores = each(lambda q, k: jnp.where(same, dot(q, k, NT), -1e30), q, k)
        weights = softmax(scores)
        rounded = weights.astype(BF)
        result = each(lambda w, o: dot(w, o, NN), rounded, o).astype(BF)
        for h in heads:
            time_mixed[:, columns[h]] = result[h * ROWS : (h + 1) * ROWS]
        d_out = jnp.concatenate([d_time[:, columns[h]] for h in heads], axis=0)
        delta = jnp.sum(d_out.astype(F32) * result.astype(F32), axis=-1, keepdims=True)
        d_weights = each(lambda d, o: dot(d, o, NT), d_out, o)
        d_scores = (weights * (d_weights - delta) * SCALE).astype(BF)
        time_d[...] = (
            each(lambda w, d: dot(w, d, TN), rounded, d_out).astype(BF).reshape(4, 4, 2, 16, HD)
        )
        d_q, product = norm_back(
            q_hat, q_factor, gain[2], each(lambda s, k: dot(s, k, NN), d_scores, k)
        )
        sums[2] += fold(product)
        time_dqk[hh, 0, pl.ds(g * 4, 4)] = d_q.reshape(4, 4, 4, 8, HD)
        d_k, product = norm_back(
            k_hat, k_factor, gain[3], each(lambda s, q: dot(s, q, TN), d_scores, q)
        )
        sums[3] += fold(product)
        time_dqk[hh, 1, pl.ds(g * 4, 4)] = d_k.reshape(4, 4, 4, 8, HD)

        for part in range(2):
            moved = dot(select[3], time_d[:, :, part].reshape(256, HD), NN).astype(BF)
            send_d[t, pl.ds(part * 16, 16)] = moved.reshape(16, 16, HD)

        def send_one(step):
            to = frame_peer(step)
            remote(send_d.at[t, to], got_d.at[g, me], d_send, d_recv.at[g], to * 2 + hh).start()

        @pl.when(hh == half)
        def _():
            pltpu.make_async_copy(send_d.at[t, frame_at], got_d.at[g, me], d_recv.at[g]).start()

        @pl.when(hh != half)
        def _():
            send_one(0)

        pl.loop(1, FRAMES)(send_one)

    mixed_out = pltpu.make_async_copy(time_mixed, mixed, mixed_sem)
    mixed_out.start()

    for hh in range(2):
        for part in range(4):
            units = [time_dqk[hh, a, :, :, part].reshape(256, HD).astype(BF) for a in range(2)]
            moved = dot(select[7], jnp.concatenate(units, axis=1), NN).astype(BF)
            for a in range(2):
                send_dqk[hh, pl.ds(part * 8, 8), :, a] = moved[:, a * HD : (a + 1) * HD].reshape(
                    8, 2, 16, HD
                )

    def nearer(frame_to):
        return ((y + 11 - 2 * (frame_to % 4)) % 8) // 4

    pltpu.make_async_copy(send_dqk.at[half, frame_at, other], got_head.at[me], head_recv).start()

    @pl.loop(1, FRAMES)
    def _(step):
        to = frame_peer(step)
        side = nearer(to)
        remote(
            send_dqk.at[side, to, 1 - side], got_head.at[me], head_send, head_recv, to * 2 + side
        ).start()

    pltpu.make_async_copy(send_dqk.at[half, frame_at, half], got_own.at[me], back_recv).start()
    remote(
        send_dqk.at[other, frame_at, other], got_own.at[me], back_send, back_recv, partner
    ).start()
    pltpu.make_async_copy(send_dqk.at[other, frame_at, half], got_token.at[me], token_recv).start()

    @pl.loop(1, FRAMES)
    def _(step):
        to = frame_peer(step)
        side = nearer(to)
        remote(
            send_dqk.at[1 - side, to, side], got_token.at[me], token_send, token_recv, to * 2 + side
        ).start()
        for hh in range(2):
            remote(
                send_dqk.at[hh, to, hh], got_own.at[me], back_send, back_recv, to * 2 + hh
            ).start()

    def out_own(a, g):
        return pltpu.make_async_copy(
            final_own.at[a, :, pl.ds(g * PART, PART)],
            outputs[a].at[:, pl.ds(half * HALF + g * PART, PART)],
            out_sem.at[a, g],
        )

    def out_trade(a, g):
        place = half * HALF + g * PART
        target = value_grad.at[:, pl.ds(place, PART)] if a == 2 else final_in.at[a, :, pl.ds(g * PART, PART)]
        return remote(
            final_out.at[a, :, pl.ds(g * PART, PART)],
            target,
            out_send.at[a, g],
            out_recv.at[a, g],
            partner,
        )

    def units_to_rows(units, block):
        here = pl.ds(block * 16, 16)
        pieces = [units[here, a].reshape(256, HD) for a in range(2)]
        return dot(select[5], jnp.concatenate(pieces, axis=1), NN)

    @pl.loop(0, 2)
    def _(g):
        wait_bytes(got_d.at[g], d_recv.at[g])

        for b in range(4):
            moved = dot(select[1], got_d[g, pl.ds(b * 16, 16)].reshape(256, HD), NN).astype(BF)
            d_space[:, :, b] = moved.reshape(4, 2, 32, HD)

        @pl.loop(0, 4)
        def _(h):
            columns = pl.ds(pl.multiple_of(g * PART + h * HD, HD), HD)
            q_hat, q_factor = hat(frame[0, :, :, columns].reshape(256, HD).astype(F32))
            k_hat, k_factor = hat(frame[1, :, :, columns].reshape(256, HD).astype(F32))
            q = (q_hat * gain[0]).astype(BF)
            k = (k_hat * gain[1]).astype(BF)
            v = frame[2, :, :, columns].reshape(256, HD)
            weights = probs[g * 4 + h]
            d_out = d_space[h].reshape(256, HD)
            result = o_space[g, h].reshape(256, HD)
            delta = jnp.sum(d_out.astype(F32) * result.astype(F32), axis=-1, keepdims=True)
            d_scores = (weights * (dot(d_out, v, NT) - delta) * SCALE).astype(BF)
            d_q, product = norm_back(q_hat, q_factor, gain[0], dot(d_scores, k, NN))
            sums[0] += fold(product)
            back[0, g * 4 + h] = d_q.reshape(2, ROWS, HD)
            d_k, product = norm_back(k_hat, k_factor, gain[1], dot(d_scores, q, TN))
            sums[1] += fold(product)
            back[1, g * 4 + h] = d_k.reshape(2, ROWS, HD)
            d_v = dot(weights.astype(BF), d_out, TN).astype(BF).reshape(2, ROWS, HD)
            final_out[2, :, columns] = lax.select(half == 0, d_v[1], d_v[0])
            final_own[2, :, columns] = lax.select(half == 0, d_v[0], d_v[1])

        out_trade(2, g).start()
        out_own(2, g).start()

    def add_units(units, r, target):
        for block in range(4):
            moved = units_to_rows(units, block)
            here = pl.ds(block * 32, 32)
            for a in range(2):
                for h in range(8):
                    total = moved[h * 32 : h * 32 + 32, a * HD : (a + 1) * HD] + back[a, h, r, here]
                    target[a, here, h * HD : (h + 1) * HD] = total.astype(BF)

    rounds = (
        (y, lambda at: {"seq": z * 32 + x * 8 + at}),
        (z * 4 + x, lambda at: {"seq": at * 8 + y}),
        (sample, lambda at: {"dp": at}),
    )

    def gather(i, total):
        place, device = rounds[i]
        gathered[i, place] = total

        @pl.loop(1, 8)
        def _(step):
            remote(
                gathered.at[i, place],
                gathered.at[i, place],
                sum_send.at[i],
                sum_recv.at[i],
                device((place + step) % 8),
            ).start()

    def gathered_sum(i):
        wait_bytes(gathered.at[i, pl.ds(0, 7)], sum_recv.at[i])
        return jnp.sum(gathered[i], axis=0)

    own = jnp.sum(sums[...], axis=1)
    gather(0, jnp.concatenate([own, jnp.zeros_like(own)], axis=0))

    wait_bytes(got_head.at[pl.ds(0, 32)], head_recv)
    add_units(got_head, other, final_out)
    for g in range(2):
        for a in range(2):
            out_trade(a, g).start()

    gather(1, gathered_sum(0))
    wait_bytes(got_own, back_recv)
    add_units(got_own, half, final_own)
    for g in range(2):
        for a in range(2):
            out_own(a, g).start()

    gather(2, gathered_sum(1))
    wait_bytes(got_token.at[pl.ds(0, 32)], token_recv)

    for g in range(2):
        for a in range(2):
            out_trade(a, g).wait_recv()

    for block in range(4):
        moved = units_to_rows(got_token, block)
        here = pl.ds(block * 32, 32)
        for a in range(2):
            for h in range(8):
                columns = slice(h * HD, (h + 1) * HD)
                total = moved[h * 32 : h * 32 + 32, a * HD : (a + 1) * HD] + final_in[
                    a, here, columns
                ].astype(F32)
                final_sum[a, here, columns] = total.astype(BF)

    sum_copies = [
        pltpu.make_async_copy(
            final_sum.at[a], outputs[a].at[:, pl.ds(other * HALF, HALF)], sum_sem.at[a]
        )
        for a in range(2)
    ]
    for copy in sum_copies:
        copy.start()
    gain_grads[...] = gathered_sum(2)[0:4]

    for i in range(3):
        wait_bytes(gathered.at[i, pl.ds(0, 7)], sum_send.at[i])
    for g in range(2):
        out_trade(2, g).wait_recv()
        for a in range(3):
            trade_copy(a, g).wait_send()
            out_trade(a, g).wait_send()
            out_own(a, g).wait()
        wait_bytes(send_o.at[g, pl.ds(0, SEQ - 1)], o_send.at[g])
    wait_bytes(send_native.at[pl.ds(0, 47)], native_send)
    wait_bytes(send_relay.at[pl.ds(0, 31)], relay_send)
    wait_bytes(got_d.at[:, pl.ds(0, SEQ - 1)], d_send)
    wait_bytes(got_head.at[pl.ds(0, 31)], head_send)
    wait_bytes(got_token.at[pl.ds(0, 31)], token_send)
    wait_bytes(got_own.at[pl.ds(0, 63)], back_send)
    mixed_out.wait()
    for copy in sum_copies:
        copy.wait()


def write_out(*refs):
    sources, targets, sem = refs[:5], refs[5:10], refs[10]
    copies = [
        pltpu.make_async_copy(source, target, sem.at[i])
        for i, (source, target) in enumerate(zip(sources, targets))
    ]
    for copy in copies:
        copy.start()
    for copy in copies:
        copy.wait()


def body(query, key, value, gains, d_mixed):
    wide = (ROWS, WIDTH)
    hbm_spec = pl.BlockSpec(memory_space=pltpu.HBM)
    any_spec = pl.BlockSpec(memory_space=pl.ANY)
    vmem_spec = pl.BlockSpec(memory_space=pltpu.VMEM)
    dma = pltpu.SemaphoreType.DMA
    shapes = [jax.ShapeDtypeStruct(wide, BF)] * 4 + [jax.ShapeDtypeStruct((4, HD), F32)]
    results = pl.pallas_call(
        kernel,
        out_shape=shapes,
        in_specs=[hbm_spec] * 5,
        out_specs=[any_spec, any_spec, any_spec, any_spec, vmem_spec],
        scratch_shapes=[
            pltpu.VMEM((4, HD), F32),
            pltpu.VMEM((len(SELECTORS), 256, 256), BF),
            pltpu.VMEM((2, ROWS, WIDTH), BF),
            pltpu.VMEM((3, 2, ROWS, HALF), BF),
            pltpu.VMEM(wide, BF),
            pltpu.VMEM((8, 256, 256), F32),
            pltpu.VMEM((2, 4, 2, 4, 32, HD), BF),
            pltpu.VMEM((SEQ, 2, 2, 16, HD), BF),
            pltpu.VMEM((SEQ, 2, 16, HD), BF),
            pltpu.VMEM((2, SEQ, 16, HD), BF),
            pltpu.VMEM((FRAMES, 2, 2, 2, 16, HD), BF),
            pltpu.VMEM((4, FRAMES, 16, HD), BF),
            pltpu.VMEM((2, 2, 8, 4, 4, 8, HD), F32),
            pltpu.VMEM((4, 4, 2, 16, HD), BF),
            pltpu.VMEM((4, 4, 2, 16, HD), BF),
            pltpu.VMEM((2, 2, 8, 4, 4, 8, HD), F32),
            pltpu.VMEM(wide, BF),
            pltpu.VMEM((4, FRAMES, 16, HD), BF),
            pltpu.VMEM((2, FRAMES, 2, 2, 16, HD), BF),
            pltpu.VMEM((2, SEQ, 16, HD), BF),
            pltpu.VMEM((SEQ, 2, 16, HD), BF),
            pltpu.VMEM((SEQ, 2, 16, HD), BF),
            pltpu.VMEM((SEQ, 2, 16, HD), BF),
            pltpu.VMEM((4, 2, 4, 32, HD), BF),
            pltpu.VMEM((2, 8, 2, ROWS, HD), F32),
            pltpu.VMEM((3, ROWS, HALF), BF),
            pltpu.VMEM((3, ROWS, HALF), BF),
            pltpu.VMEM((2, ROWS, HALF), BF),
            pltpu.VMEM((2, ROWS, HALF), BF),
            pltpu.VMEM((4, 8, HD), F32),
            pltpu.VMEM((3, 8, 8, HD), F32),
            dma,
            dma((2,)),
            dma((3, 2)),
            dma((3, 2)),
            dma((3, 2)),
            dma,
            dma,
            dma,
            dma,
            dma,
            dma((2,)),
            dma((4,)),
            dma,
            dma((2,)),
            dma,
            dma,
            dma,
            dma,
            dma,
            dma,
            dma((3, 2)),
            dma((3, 2)),
            dma((3, 2)),
            dma((2,)),
            dma((3,)),
            dma((3,)),
        ],
        compiler_params=pltpu.CompilerParams(
            collective_id=0, has_side_effects=True, vmem_limit_bytes=103 * 2**19
        ),
        cost_estimate=pl.CostEstimate(flops=2 * 10**9, bytes_accessed=2**22, transcendentals=10**6),
        name="space_time_attention",
    )(query.reshape(wide), key.reshape(wide), value.reshape(wide), gains, d_mixed.reshape(wide))
    mixed, query_grad, key_grad, value_grad, gain_grads = pl.pallas_call(
        write_out,
        out_shape=shapes,
        in_specs=[vmem_spec] * 5,
        out_specs=[hbm_spec] * 5,
        scratch_shapes=[dma((5,))],
        compiler_params=pltpu.CompilerParams(vmem_limit_bytes=4 * 2**20),
        name="write_out",
    )(*results)
    return (
        mixed.reshape(d_mixed.shape),
        query_grad.reshape(query.shape),
        key_grad.reshape(key.shape),
        value_grad.reshape(value.shape),
        gain_grads,
    )


def solution(mesh):
    placed = (
        P("dp", "seq", None),
        P("dp", "seq", None),
        P("dp", "seq", None),
        P(),
        P("dp", None, "seq", None, None),
    )
    return jax.shard_map(
        body,
        mesh=mesh,
        in_specs=placed,
        out_specs=(
            P("dp", None, "seq", None, None),
            P("dp", "seq", None),
            P("dp", "seq", None),
            P("dp", "seq", None),
            P(),
        ),
        check_vma=False,
    )
```

```python
import jax
import jax.numpy as jnp
from jax import lax
from jax.experimental import pallas as pl
from jax.experimental.pallas import tpu as pltpu
from jax.sharding import PartitionSpec as P

SEQ = 64
DP = 8
WIDTH = 2048
HALF = 1024
PART = 512
HD = 128
ROWS = 128
FRAMES = 32
EPS = 1e-06
SCALE = HD**-0.5
SCALE2 = SCALE * 1.4426950408889634
BF = jnp.bfloat16
F32 = jnp.float32


def dot(a, b, dims):
    return lax.dot_general(a, b, (dims, ((), ())), preferred_element_type=F32)


NN = ((1,), (0,))
NT = ((1,), (1,))
TN = ((0,), (0,))


def selector(column_of_row):
    row = lax.broadcasted_iota(jnp.int32, (256, 256), 0)
    column = lax.broadcasted_iota(jnp.int32, (256, 256), 1)
    return jnp.where(column == column_of_row(row), 1.0, 0.0).astype(BF)


def from_space(o):
    return (o & 3) * 64 + ((o >> 2) & 1) * 32 + (o >> 4) * 2 + ((o >> 3) & 1)


def to_space(i):
    return ((i & 31) >> 1) * 16 + (i & 1) * 8 + ((i >> 5) & 1) * 4 + (i >> 6)


def to_time(o):
    return (o & 15) * 16 + ((o >> 4) & 1) * 8 + ((o >> 5) & 1) * 4 + (o >> 6)


def from_time(i):
    return (i & 3) * 64 + (((i >> 2) & 1) * 2 + ((i >> 3) & 1)) * 16 + (i >> 4)


def from_rows(o):
    return (o & 7) * 32 + (o >> 4) * 2 + ((o >> 3) & 1)


def to_rows(i):
    return ((i & 31) >> 1) * 16 + (i & 1) * 8 + (i >> 5)


def to_time8(o):
    return (o & 7) * 32 + ((o >> 4) & 1) * 16 + ((o >> 3) & 1) * 8 + (o >> 5)


def from_time8(c):
    return (c & 7) * 32 + (((c >> 4) & 1) * 2 + ((c >> 3) & 1)) * 8 + (c >> 5)


SELECTORS = (from_space, to_space, to_time, from_time, from_rows, to_rows, to_time8, from_time8)


def hat(values):
    factor = lax.rsqrt(jnp.sum(values * values, axis=-1, keepdims=True) * (1.0 / HD) + EPS)
    return values * factor, factor


def softmax(scores):
    peak = jnp.max(scores, axis=-1, keepdims=True)
    raised = jnp.exp2((scores - peak) * SCALE2)
    return raised * (1.0 / jnp.sum(raised, axis=-1, keepdims=True))


def norm_back(x_hat, factor, gain, incoming):
    product = incoming * x_hat
    mean = jnp.sum(product * gain, axis=-1, keepdims=True) * (1.0 / HD)
    return factor * (incoming * gain - x_hat * mean), product


def fold(product):
    return jnp.sum(product.reshape(-1, 8, HD), axis=0)


def kernel(
    query, key, value, gains_in, d_mixed,
    mixed, query_grad, key_grad, value_grad, gain_grads,
    gains, select, native, frame, d_time, probs, o_space, send_native, send_relay, send_o, got_qk, got_o,
    time_qk, time_o, time_d, time_dqk, time_mixed, send_d, send_dqk, got_d, got_own, got_cross,
    d_space, back, final_out, final_own, final_in, final_sum, sums, gathered,
    gains_sem, native_sem, own_sem, trade_send, trade_recv, mixed_in_sem, mixed_sem,
    native_send, relay_send, qk_recv, o_send, o_recv, d_send, d_recv,
    cross_send, back_send, cross_recv, back_recv,
    out_sem, out_send, out_recv, sum_sem, sum_send, sum_recv,
):
    me = lax.axis_index("seq")
    sample = lax.axis_index("dp")
    z, x, y = me // 32, (me // 8) % 4, me % 8
    half, frame_at = me % 2, me // 2
    other = 1 - half
    partner = me + 1 - 2 * half

    def device_at(step, dy):
        return ((z + step // 16) % 2) * 32 + ((x + (step // 4) % 4) % 4) * 8 + (y + 8 + dy) % 8

    def peer(step):
        return (
            ((z + step // 32) % 2) * 32 + ((x + (step // 8) % 4) % 4) * 8 + (y + step % 8) % 8
        )

    def near_peer(step):
        return device_at(step, (step % 4) * (2 * half - 1))

    def far_peer(step):
        return device_at(step, (step % 4 + 1) * (1 - 2 * half))

    def frame_peer(step):
        return (
            ((z + step // 16) % 2) * 16
            + ((x + (step // 4) % 4) % 4) * 4
            + (y // 2 + step % 4) % 4
        )

    def remote(source, target, send_sem, recv_sem, to):
        return pltpu.make_async_remote_copy(
            src_ref=source,
            dst_ref=target,
            send_sem=send_sem,
            recv_sem=recv_sem,
            device_id=to if isinstance(to, dict) else {"seq": to},
            device_id_type=pl.DeviceIdType.MESH,
        )

    def wait_bytes(ref, sem):
        pltpu.make_async_copy(ref, ref, sem).wait()

    inputs = (query, key, value)
    outputs = (query_grad, key_grad, value_grad)

    def own_copy(a, g):
        return pltpu.make_async_copy(
            inputs[a].at[:, pl.ds(half * HALF + g * PART, PART)],
            frame.at[a, half, :, pl.ds(g * PART, PART)],
            own_sem.at[a, g],
        )

    def trade_copy(a, g):
        return remote(
            inputs[a].at[:, pl.ds(other * HALF + g * PART, PART)],
            frame.at[a, half, :, pl.ds(g * PART, PART)],
            trade_send.at[a, g],
            trade_recv.at[a, g],
            partner,
        )

    gains_copy = pltpu.make_async_copy(gains_in, gains, gains_sem)
    gains_copy.start()
    native_copies = [
        pltpu.make_async_copy(inputs[a], native.at[a], native_sem.at[a]) for a in range(2)
    ]
    for copy in native_copies:
        copy.start()
    for g in range(2):
        for a in range(3):
            own_copy(a, g).start()
    mixed_in = pltpu.make_async_copy(d_mixed, d_time, mixed_in_sem)
    mixed_in.start()
    got_cross[...] = jnp.zeros_like(got_cross)

    barrier = pltpu.get_barrier_semaphore()

    @pl.loop(1, SEQ)
    def _(step):
        pl.semaphore_signal(
            barrier, inc=1, device_id={"seq": peer(step)}, device_id_type=pl.DeviceIdType.MESH
        )

    @pl.loop(1, DP)
    def _(step):
        pl.semaphore_signal(
            barrier,
            inc=1,
            device_id={"dp": (sample + step) % DP},
            device_id_type=pl.DeviceIdType.MESH,
        )

    pl.semaphore_wait(barrier, SEQ - 1 + DP - 1)

    for g in range(2):
        for a in range(3):
            trade_copy(a, g).start()

    for i, source in enumerate(SELECTORS):
        select[i] = selector(source)
    sums[...] = jnp.zeros_like(sums)
    gains_copy.wait()
    gain = [gains[i : i + 1, :] for i in range(4)]

    def rows_to_units(source, block, first, target):
        pieces = [
            jnp.concatenate(
                [source(a)[pl.ds(block * 32, 32), pl.ds(first + h * HD, HD)] for h in range(8)], axis=0
            )
            for a in range(2)
        ]
        moved = dot(select[4], jnp.concatenate(pieces, axis=1), NN).astype(BF)
        for a in range(2):
            target(pl.ds(block * 16, 16), a, moved[:, a * HD : (a + 1) * HD].reshape(16, 16, HD))

    for copy in native_copies:
        copy.wait()

    for hh in range(2):

        def put(devices, a, units):
            send_native[devices, hh, a] = units

        for block in range(4):
            rows_to_units(lambda a: native.at[a], block, hh * HALF, put)

    pltpu.make_async_copy(send_native.at[me], got_qk.at[frame_at, half], qk_recv).start()

    @pl.loop(1, 32)
    def _(step):
        to = near_peer(step)
        remote(send_native.at[to], got_qk.at[frame_at, half], native_send, qk_recv, to).start()

    @pl.loop(0, 2)
    def _(g):
        for a in range(3):
            own_copy(a, g).wait()
            trade_copy(a, g).wait_recv()

        @pl.when(g == 1)
        def _():
            def put_relay(devices, a, units):
                send_relay[devices, a] = units

            for block in range(4):
                rows_to_units(lambda a: frame.at[a, other], block, 0, put_relay)

            pltpu.make_async_copy(send_relay.at[me], got_qk.at[frame_at, other, half], qk_recv).start()

            @pl.loop(1, 32)
            def _(step):
                to = near_peer(step)
                remote(
                    send_relay.at[to], got_qk.at[frame_at, other, half], relay_send, qk_recv, to
                ).start()

        @pl.when(g == 0)
        def _():
            @pl.loop(0, 32)
            def _(step):
                to = far_peer(step)
                remote(
                    send_native.at[to, half], got_qk.at[frame_at, half, half], native_send, qk_recv, to
                ).start()

        @pl.loop(0, 4)
        def _(h):
            columns = pl.ds(pl.multiple_of(g * PART + h * HD, HD), HD)
            q_hat, _ = hat(frame[0, :, :, columns].reshape(256, HD).astype(F32))
            k_hat, _ = hat(frame[1, :, :, columns].reshape(256, HD).astype(F32))
            q = (q_hat * gain[0]).astype(BF)
            k = (k_hat * gain[1]).astype(BF)
            weights = softmax(dot(q, k, NT))
            probs[g * 4 + h] = weights
            result = dot(weights.astype(BF), frame[2, :, :, columns].reshape(256, HD), NN)
            o_space[g, h] = result.astype(BF).reshape(2, 4, 32, HD)

        for b in range(4):
            moved = dot(select[0], o_space[g, :, :, b].reshape(256, HD), NN).astype(BF)
            send_o[g, pl.ds(b * 16, 16)] = moved.reshape(16, 16, HD)

        slot = g * 2 + half
        pltpu.make_async_copy(send_o.at[g, me], got_o.at[slot, frame_at], o_recv.at[slot]).start()

        @pl.loop(1, SEQ)
        def _(step):
            to = peer(step)
            remote(
                send_o.at[g, to], got_o.at[slot, frame_at], o_send.at[g], o_recv.at[slot], to
            ).start()

    def send_cross(hh):
        for part in range(4):
            units = [time_dqk[hh, a, :, :, part].reshape(256, HD).astype(BF) for a in range(2)]
            moved = dot(select[7], jnp.concatenate(units, axis=1), NN).astype(BF)
            for a in range(2):
                send_dqk[hh, pl.ds(part * 8, 8), :, a] = moved[:, a * HD : (a + 1) * HD].reshape(
                    8, 2, 16, HD
                )
        own_kind = half if hh == 0 else 1 - half
        pltpu.make_async_copy(
            send_dqk.at[hh, frame_at, 1 - hh], got_cross.at[own_kind, me], cross_recv.at[own_kind]
        ).start()

        @pl.loop(1, FRAMES)
        def _(step):
            to = frame_peer(step)
            side = ((y + 11 - 2 * (to % 4)) % 8) // 4
            kind = side if hh == 0 else 1 - side
            remote(
                send_dqk.at[hh, to, 1 - hh],
                got_cross.at[kind, me],
                cross_send,
                cross_recv.at[kind],
                to * 2 + side,
            ).start()

    wait_bytes(got_qk, qk_recv)
    for hh in range(2):
        for part in range(4):
            here = pl.ds(part * 8, 8)
            units = [got_qk[here, :, hh, a].reshape(256, HD) for a in range(2)]
            moved = dot(select[6], jnp.concatenate(units, axis=1), NN)
            for a in range(2):
                time_qk[hh, a, :, :, part] = moved[:, a * HD : (a + 1) * HD].reshape(8, 4, 8, HD)

    mixed_in.wait()
    group = lax.broadcasted_iota(jnp.int32, (ROWS, ROWS), 0) // FRAMES
    same = group == lax.broadcasted_iota(jnp.int32, (ROWS, ROWS), 1) // FRAMES

    @pl.loop(0, 4)
    def _(t):
        hh = t % 2
        g = t // 2
        wait_bytes(got_o.at[t], o_recv.at[t])
        for part in range(2):
            units = got_o[t, pl.ds(part * 16, 16)].reshape(256, HD)
            time_o[:, :, part] = dot(select[2], units, NN).astype(BF).reshape(4, 4, 16, HD)

        heads = range(4)

        def each(one, *stacked):
            return jnp.concatenate(
                [one(*(values[h * ROWS : (h + 1) * ROWS] for values in stacked)) for h in heads], axis=0
            )

        columns = [
            pl.ds(pl.multiple_of(hh * HALF + g * PART + h * HD, HD), HD) for h in heads
        ]
        q_hat, q_factor = hat(time_qk[hh, 0, pl.ds(g * 4, 4)].reshape(4 * ROWS, HD))
        k_hat, k_factor = hat(time_qk[hh, 1, pl.ds(g * 4, 4)].reshape(4 * ROWS, HD))
        o = time_o[...].reshape(4 * ROWS, HD)
        q = (q_hat * gain[2]).astype(BF)
        k = (k_hat * gain[3]).astype(BF)
        scores = each(lambda q, k: jnp.where(same, dot(q, k, NT), -1e30), q, k)
        weights = softmax(scores)
        rounded = weights.astype(BF)
        result = each(lambda w, o: dot(w, o, NN), rounded, o).astype(BF)
        for h in heads:
            time_mixed[:, columns[h]] = result[h * ROWS : (h + 1) * ROWS]
        d_out = jnp.concatenate([d_time[:, columns[h]] for h in heads], axis=0)
        delta = jnp.sum(d_out.astype(F32) * result.astype(F32), axis=-1, keepdims=True)
        d_weights = each(lambda d, o: dot(d, o, NT), d_out, o)
        d_scores = (weights * (d_weights - delta) * SCALE).astype(BF)
        time_d[...] = (
            each(lambda w, d: dot(w, d, TN), rounded, d_out).astype(BF).reshape(4, 4, 2, 16, HD)
        )
        d_q, product = norm_back(
            q_hat, q_factor, gain[2], each(lambda s, k: dot(s, k, NN), d_scores, k)
        )
        sums[2] += fold(product)
        time_dqk[hh, 0, pl.ds(g * 4, 4)] = d_q.reshape(4, 4, 4, 8, HD)
        d_k, product = norm_back(
            k_hat, k_factor, gain[3], each(lambda s, q: dot(s, q, TN), d_scores, q)
        )
        sums[3] += fold(product)
        time_dqk[hh, 1, pl.ds(g * 4, 4)] = d_k.reshape(4, 4, 4, 8, HD)

        for part in range(2):
            moved = dot(select[3], time_d[:, :, part].reshape(256, HD), NN).astype(BF)
            send_d[t, pl.ds(part * 16, 16)] = moved.reshape(16, 16, HD)

        def send_one(step):
            to = frame_peer(step)
            remote(send_d.at[t, to], got_d.at[g, me], d_send, d_recv.at[g], to * 2 + hh).start()

        @pl.when(hh == half)
        def _():
            pltpu.make_async_copy(send_d.at[t, frame_at], got_d.at[g, me], d_recv.at[g]).start()

        @pl.when(hh != half)
        def _():
            send_one(0)

        pl.loop(1, FRAMES)(send_one)

        @pl.when(t == 2)
        def _():
            send_cross(0)

    mixed_out = pltpu.make_async_copy(time_mixed, mixed, mixed_sem)
    mixed_out.start()

    send_cross(1)
    pltpu.make_async_copy(send_dqk.at[half, frame_at, half], got_own.at[me], back_recv).start()
    remote(
        send_dqk.at[other, frame_at, other], got_own.at[me], back_send, back_recv, partner
    ).start()

    @pl.loop(1, FRAMES)
    def _(step):
        to = frame_peer(step)
        for hh in range(2):
            remote(
                send_dqk.at[hh, to, hh], got_own.at[me], back_send, back_recv, to * 2 + hh
            ).start()

    def out_own(a, g):
        return pltpu.make_async_copy(
            final_own.at[a, :, pl.ds(g * PART, PART)],
            outputs[a].at[:, pl.ds(half * HALF + g * PART, PART)],
            out_sem.at[a, g],
        )

    def out_trade(a, g):
        place = half * HALF + g * PART
        target = value_grad.at[:, pl.ds(place, PART)] if a == 2 else final_in.at[a, :, pl.ds(g * PART, PART)]
        return remote(
            final_out.at[a, :, pl.ds(g * PART, PART)],
            target,
            out_send.at[a, g],
            out_recv.at[a, g],
            partner,
        )

    def units_to_rows(units, block):
        here = pl.ds(block * 16, 16)
        pieces = [units[here, a].reshape(256, HD) for a in range(2)]
        return dot(select[5], jnp.concatenate(pieces, axis=1), NN)

    @pl.loop(0, 2)
    def _(g):
        wait_bytes(got_d.at[g], d_recv.at[g])

        for b in range(4):
            moved = dot(select[1], got_d[g, pl.ds(b * 16, 16)].reshape(256, HD), NN).astype(BF)
            d_space[:, :, b] = moved.reshape(4, 2, 32, HD)

        @pl.loop(0, 4)
        def _(h):
            columns = pl.ds(pl.multiple_of(g * PART + h * HD, HD), HD)
            q_hat, q_factor = hat(frame[0, :, :, columns].reshape(256, HD).astype(F32))
            k_hat, k_factor = hat(frame[1, :, :, columns].reshape(256, HD).astype(F32))
            q = (q_hat * gain[0]).astype(BF)
            k = (k_hat * gain[1]).astype(BF)
            v = frame[2, :, :, columns].reshape(256, HD)
            weights = probs[g * 4 + h]
            d_out = d_space[h].reshape(256, HD)
            result = o_space[g, h].reshape(256, HD)
            delta = jnp.sum(d_out.astype(F32) * result.astype(F32), axis=-1, keepdims=True)
            d_scores = (weights * (dot(d_out, v, NT) - delta) * SCALE).astype(BF)
            d_q, product = norm_back(q_hat, q_factor, gain[0], dot(d_scores, k, NN))
            sums[0] += fold(product)
            back[0, g * 4 + h] = d_q.reshape(2, ROWS, HD)
            d_k, product = norm_back(k_hat, k_factor, gain[1], dot(d_scores, q, TN))
            sums[1] += fold(product)
            back[1, g * 4 + h] = d_k.reshape(2, ROWS, HD)
            d_v = dot(weights.astype(BF), d_out, TN).astype(BF).reshape(2, ROWS, HD)
            final_out[2, :, columns] = lax.select(half == 0, d_v[1], d_v[0])
            final_own[2, :, columns] = lax.select(half == 0, d_v[0], d_v[1])

        out_trade(2, g).start()
        out_own(2, g).start()

    def add_units(units, r, target):
        for block in range(4):
            moved = units_to_rows(units, block)
            here = pl.ds(block * 32, 32)
            for a in range(2):
                for h in range(8):
                    total = moved[h * 32 : h * 32 + 32, a * HD : (a + 1) * HD] + back[a, h, r, here]
                    target[a, here, h * HD : (h + 1) * HD] = total.astype(BF)

    rounds = (
        (y, lambda at: {"seq": z * 32 + x * 8 + at}),
        (z * 4 + x, lambda at: {"seq": at * 8 + y}),
        (sample, lambda at: {"dp": at}),
    )

    def gather(i, total):
        place, device = rounds[i]
        gathered[i, place] = total

        @pl.loop(1, 8)
        def _(step):
            remote(
                gathered.at[i, place],
                gathered.at[i, place],
                sum_send.at[i],
                sum_recv.at[i],
                device((place + step) % 8),
            ).start()

    def gathered_sum(i):
        wait_bytes(gathered.at[i, pl.ds(0, 7)], sum_recv.at[i])
        return jnp.sum(gathered[i], axis=0)

    own = jnp.sum(sums[...], axis=1)
    gather(0, jnp.concatenate([own, jnp.zeros_like(own)], axis=0))

    wait_bytes(got_cross.at[0, pl.ds(0, 32)], cross_recv.at[0])
    add_units(got_cross.at[0], other, final_out)
    gather(1, gathered_sum(0))
    for a in range(2):
        for g in range(2):
            out_trade(a, g).start()

    gather(2, gathered_sum(1))
    wait_bytes(got_own, back_recv)
    add_units(got_own, half, final_own)
    for g in range(2):
        for a in range(2):
            out_own(a, g).start()

    wait_bytes(got_cross.at[1, pl.ds(0, 32)], cross_recv.at[1])

    def sum_copy(a):
        return pltpu.make_async_copy(
            final_sum.at[a], outputs[a].at[:, pl.ds(other * HALF, HALF)], sum_sem.at[a]
        )

    added = [units_to_rows(got_cross.at[1], block) for block in range(4)]
    for a in range(2):
        for g in range(2):
            out_trade(a, g).wait_recv()
        for block in range(4):
            here = pl.ds(block * 32, 32)
            for h in range(8):
                columns = slice(h * HD, (h + 1) * HD)
                total = added[block][h * 32 : h * 32 + 32, a * HD : (a + 1) * HD] + final_in[
                    a, here, columns
                ].astype(F32)
                final_sum[a, here, columns] = total.astype(BF)
        sum_copy(a).start()
    gain_grads[...] = gathered_sum(2)[0:4]

    for i in range(3):
        wait_bytes(gathered.at[i, pl.ds(0, 7)], sum_send.at[i])
    for g in range(2):
        out_trade(2, g).wait_recv()
        for a in range(3):
            trade_copy(a, g).wait_send()
            out_trade(a, g).wait_send()
            out_own(a, g).wait()
        wait_bytes(send_o.at[g, pl.ds(0, SEQ - 1)], o_send.at[g])
    wait_bytes(send_native.at[pl.ds(0, 47)], native_send)
    wait_bytes(send_relay.at[pl.ds(0, 31)], relay_send)
    wait_bytes(got_d.at[:, pl.ds(0, SEQ - 1)], d_send)
    wait_bytes(got_cross.at[:, pl.ds(0, 31)], cross_send)
    wait_bytes(got_own.at[pl.ds(0, 63)], back_send)
    mixed_out.wait()
    for a in range(2):
        sum_copy(a).wait()


def write_out(*refs):
    sources, targets, sem = refs[:5], refs[5:10], refs[10]
    copies = [
        pltpu.make_async_copy(source, target, sem.at[i])
        for i, (source, target) in enumerate(zip(sources, targets))
    ]
    for copy in copies:
        copy.start()
    for copy in copies:
        copy.wait()


def body(query, key, value, gains, d_mixed):
    wide = (ROWS, WIDTH)
    hbm_spec = pl.BlockSpec(memory_space=pltpu.HBM)
    any_spec = pl.BlockSpec(memory_space=pl.ANY)
    vmem_spec = pl.BlockSpec(memory_space=pltpu.VMEM)
    dma = pltpu.SemaphoreType.DMA
    shapes = [jax.ShapeDtypeStruct(wide, BF)] * 4 + [jax.ShapeDtypeStruct((4, HD), F32)]
    results = pl.pallas_call(
        kernel,
        out_shape=shapes,
        in_specs=[hbm_spec] * 5,
        out_specs=[any_spec, any_spec, any_spec, any_spec, vmem_spec],
        scratch_shapes=[
            pltpu.VMEM((4, HD), F32),
            pltpu.VMEM((len(SELECTORS), 256, 256), BF),
            pltpu.VMEM((2, ROWS, WIDTH), BF),
            pltpu.VMEM((3, 2, ROWS, HALF), BF),
            pltpu.VMEM(wide, BF),
            pltpu.VMEM((8, 256, 256), F32),
            pltpu.VMEM((2, 4, 2, 4, 32, HD), BF),
            pltpu.VMEM((SEQ, 2, 2, 16, HD), BF),
            pltpu.VMEM((SEQ, 2, 16, HD), BF),
            pltpu.VMEM((2, SEQ, 16, HD), BF),
            pltpu.VMEM((FRAMES, 2, 2, 2, 16, HD), BF),
            pltpu.VMEM((4, FRAMES, 16, HD), BF),
            pltpu.VMEM((2, 2, 8, 4, 4, 8, HD), F32),
            pltpu.VMEM((4, 4, 2, 16, HD), BF),
            pltpu.VMEM((4, 4, 2, 16, HD), BF),
            pltpu.VMEM((2, 2, 8, 4, 4, 8, HD), F32),
            pltpu.VMEM(wide, BF),
            pltpu.VMEM((4, FRAMES, 16, HD), BF),
            pltpu.VMEM((2, FRAMES, 2, 2, 16, HD), BF),
            pltpu.VMEM((2, SEQ, 16, HD), BF),
            pltpu.VMEM((SEQ, 2, 16, HD), BF),
            pltpu.VMEM((2, SEQ, 2, 16, HD), BF),
            pltpu.VMEM((4, 2, 4, 32, HD), BF),
            pltpu.VMEM((2, 8, 2, ROWS, HD), F32),
            pltpu.VMEM((3, ROWS, HALF), BF),
            pltpu.VMEM((3, ROWS, HALF), BF),
            pltpu.VMEM((2, ROWS, HALF), BF),
            pltpu.VMEM((2, ROWS, HALF), BF),
            pltpu.VMEM((4, 8, HD), F32),
            pltpu.VMEM((3, 8, 8, HD), F32),
            dma,
            dma((2,)),
            dma((3, 2)),
            dma((3, 2)),
            dma((3, 2)),
            dma,
            dma,
            dma,
            dma,
            dma,
            dma((2,)),
            dma((4,)),
            dma,
            dma((2,)),
            dma,
            dma,
            dma((2,)),
            dma,
            dma((3, 2)),
            dma((3, 2)),
            dma((3, 2)),
            dma((2,)),
            dma((3,)),
            dma((3,)),
        ],
        compiler_params=pltpu.CompilerParams(
            collective_id=0, has_side_effects=True, vmem_limit_bytes=103 * 2**19
        ),
        cost_estimate=pl.CostEstimate(flops=2 * 10**9, bytes_accessed=2**22, transcendentals=10**6),
        name="space_time_attention",
    )(query.reshape(wide), key.reshape(wide), value.reshape(wide), gains, d_mixed.reshape(wide))
    mixed, query_grad, key_grad, value_grad, gain_grads = pl.pallas_call(
        write_out,
        out_shape=shapes,
        in_specs=[vmem_spec] * 5,
        out_specs=[hbm_spec] * 5,
        scratch_shapes=[dma((5,))],
        compiler_params=pltpu.CompilerParams(vmem_limit_bytes=4 * 2**20),
        name="write_out",
    )(*results)
    return (
        mixed.reshape(d_mixed.shape),
        query_grad.reshape(query.shape),
        key_grad.reshape(key.shape),
        value_grad.reshape(value.shape),
        gain_grads,
    )


def solution(mesh):
    placed = (
        P("dp", "seq", None),
        P("dp", "seq", None),
        P("dp", "seq", None),
        P(),
        P("dp", None, "seq", None, None),
    )
    return jax.shard_map(
        body,
        mesh=mesh,
        in_specs=placed,
        out_specs=(
            P("dp", None, "seq", None, None),
            P("dp", "seq", None),
            P("dp", "seq", None),
            P("dp", "seq", None),
            P(),
        ),
        check_vma=False,
    )
```

```python
import jax
import jax.numpy as jnp
from jax import lax
from jax.experimental import pallas as pl
from jax.experimental.pallas import tpu as pltpu
from jax.sharding import PartitionSpec as P

SEQ = 64
DP = 8
WIDTH = 2048
HALF = 1024
PART = 512
HD = 128
ROWS = 128
FRAMES = 32
EPS = 1e-06
SCALE = HD**-0.5
SCALE2 = SCALE * 1.4426950408889634
BF = jnp.bfloat16
F32 = jnp.float32


def dot(a, b, dims):
    return lax.dot_general(a, b, (dims, ((), ())), preferred_element_type=F32)


NN = ((1,), (0,))
NT = ((1,), (1,))
TN = ((0,), (0,))


def selector(column_of_row):
    row = lax.broadcasted_iota(jnp.int32, (256, 256), 0)
    column = lax.broadcasted_iota(jnp.int32, (256, 256), 1)
    return jnp.where(column == column_of_row(row), 1.0, 0.0).astype(BF)


def from_space(o):
    return (o & 3) * 64 + ((o >> 2) & 1) * 32 + (o >> 4) * 2 + ((o >> 3) & 1)


def to_space(i):
    return ((i & 31) >> 1) * 16 + (i & 1) * 8 + ((i >> 5) & 1) * 4 + (i >> 6)


def to_time(o):
    return (o & 15) * 16 + ((o >> 4) & 1) * 8 + ((o >> 5) & 1) * 4 + (o >> 6)


def from_time(i):
    return (i & 3) * 64 + (((i >> 2) & 1) * 2 + ((i >> 3) & 1)) * 16 + (i >> 4)


def from_rows(o):
    return (o & 7) * 32 + (o >> 4) * 2 + ((o >> 3) & 1)


def to_rows(i):
    return ((i & 31) >> 1) * 16 + (i & 1) * 8 + (i >> 5)


def to_time8(o):
    return (o & 7) * 32 + ((o >> 4) & 1) * 16 + ((o >> 3) & 1) * 8 + (o >> 5)


def from_time8(c):
    return (c & 7) * 32 + (((c >> 4) & 1) * 2 + ((c >> 3) & 1)) * 8 + (c >> 5)


SELECTORS = (from_space, to_space, to_time, from_time, from_rows, to_rows, to_time8, from_time8)


def hat(values):
    factor = lax.rsqrt(jnp.sum(values * values, axis=-1, keepdims=True) * (1.0 / HD) + EPS)
    return values * factor, factor


def softmax(scores):
    peak = jnp.max(scores, axis=-1, keepdims=True)
    raised = jnp.exp2((scores - peak) * SCALE2)
    return raised * (1.0 / jnp.sum(raised, axis=-1, keepdims=True))


def norm_back(x_hat, factor, gain, incoming):
    product = incoming * x_hat
    mean = jnp.sum(product * gain, axis=-1, keepdims=True) * (1.0 / HD)
    return factor * (incoming * gain - x_hat * mean), product


def fold(product):
    return jnp.sum(product.reshape(-1, 8, HD), axis=0)


def kernel(
    query, key, value, gains_in, d_mixed,
    mixed, query_grad, key_grad, value_grad, gain_grads,
    gains, select, native, frame, d_time, probs, o_space, send_native, send_relay, send_o, got_qk, got_o,
    time_qk, time_o, time_d, time_dqk, time_mixed, send_d, send_dqk, got_d, got_own, got_cross,
    d_space, back, final_out, final_own, final_in, sums, gathered,
    gains_sem, native_sem, own_sem, trade_send, trade_recv, mixed_in_sem, mixed_sem,
    native_send, relay_send, qk_recv, o_send, o_recv, d_send, d_recv,
    cross_send, back_send, cross_recv, back_recv,
    out_sem, out_send, out_recv, sum_send, sum_recv,
):
    me = lax.axis_index("seq")
    sample = lax.axis_index("dp")
    z, x, y = me // 32, (me // 8) % 4, me % 8
    half, frame_at = me % 2, me // 2
    other = 1 - half
    partner = me + 1 - 2 * half

    def each_peer(one):
        @pl.loop(1, 8)
        def _(at):
            base = ((z + (8 - at) // 4) % 2) * 32 + ((x + (8 - at) % 4) % 4) * 8
            for dy in (4, 3, 5, 2, 6, 1, 7, 0):
                one(base + (y + dy) % 8)

        for dy in (4, 3, 5, 2, 6, 1, 7):
            one(z * 32 + x * 8 + (y + dy) % 8)

    def each_frame(one):
        @pl.loop(1, 8)
        def _(at):
            base = ((z + (8 - at) // 4) % 2) * 16 + ((x + (8 - at) % 4) % 4) * 4
            for dy in (2, 1, 3, 0):
                one(base + (y // 2 + dy) % 4)

        for dy in (2, 1, 3):
            one(z * 16 + x * 4 + (y // 2 + dy) % 4)

    away = 2 * half - 1

    def each_near(one):
        @pl.loop(1, 8)
        def _(at):
            base = ((z + (8 - at) // 4) % 2) * 32 + ((x + (8 - at) % 4) % 4) * 8
            for dy in (3, 2, 1, 0):
                one(base + (y + 8 + dy * away) % 8)

        for dy in (3, 2, 1):
            one(z * 32 + x * 8 + (y + 8 + dy * away) % 8)

    def each_far(one):
        @pl.loop(0, 8)
        def _(at):
            base = ((z + (7 - at) // 4) % 2) * 32 + ((x + (7 - at) % 4) % 4) * 8
            for dy in (4, 3, 2, 1):
                one(base + (y + 8 - dy * away) % 8)

    def remote(source, target, send_sem, recv_sem, to):
        return pltpu.make_async_remote_copy(
            src_ref=source,
            dst_ref=target,
            send_sem=send_sem,
            recv_sem=recv_sem,
            device_id=to if isinstance(to, dict) else {"seq": to},
            device_id_type=pl.DeviceIdType.MESH,
        )

    def wait_bytes(ref, sem):
        pltpu.make_async_copy(ref, ref, sem).wait()

    inputs = (query, key, value)
    outputs = (query_grad, key_grad, value_grad)

    def own_copy(a, g):
        return pltpu.make_async_copy(
            inputs[a].at[:, pl.ds(half * HALF + g * PART, PART)],
            frame.at[a, half, :, pl.ds(g * PART, PART)],
            own_sem.at[a, g],
        )

    def trade_copy(a, g):
        return remote(
            inputs[a].at[:, pl.ds(other * HALF + g * PART, PART)],
            frame.at[a, half, :, pl.ds(g * PART, PART)],
            trade_send.at[a, g],
            trade_recv.at[a, g],
            partner,
        )

    gains_copy = pltpu.make_async_copy(gains_in, gains, gains_sem)
    gains_copy.start()
    native_copies = [
        pltpu.make_async_copy(inputs[a], native.at[a], native_sem.at[a]) for a in range(2)
    ]
    for copy in native_copies:
        copy.start()
    for g in range(2):
        for a in range(3):
            own_copy(a, g).start()
    mixed_in = pltpu.make_async_copy(d_mixed, d_time, mixed_in_sem)
    mixed_in.start()
    got_cross[...] = jnp.zeros_like(got_cross)

    barrier = pltpu.get_barrier_semaphore()

    @pl.loop(1, DP)
    def _(step):
        pl.semaphore_signal(
            barrier,
            inc=1,
            device_id={"dp": (sample + step) % DP},
            device_id_type=pl.DeviceIdType.MESH,
        )

    each_peer(
        lambda to: pl.semaphore_signal(
            barrier, inc=1, device_id={"seq": to}, device_id_type=pl.DeviceIdType.MESH
        )
    )

    pl.semaphore_wait(barrier, SEQ - 1 + DP - 1)

    for g in range(2):
        for a in range(3):
            trade_copy(a, g).start()

    for i, source in enumerate(SELECTORS):
        select[i] = selector(source)
    sums[...] = jnp.zeros_like(sums)
    gains_copy.wait()
    gain = [gains[i : i + 1, :] for i in range(4)]

    def rows_to_units(source, block, first, target):
        pieces = [
            jnp.concatenate(
                [source(a)[pl.ds(block * 32, 32), pl.ds(first + h * HD, HD)] for h in range(8)], axis=0
            )
            for a in range(2)
        ]
        moved = dot(select[4], jnp.concatenate(pieces, axis=1), NN).astype(BF)
        for a in range(2):
            target(pl.ds(block * 16, 16), a, moved[:, a * HD : (a + 1) * HD].reshape(16, 16, HD))

    for copy in native_copies:
        copy.wait()

    for hh in range(2):

        def put(devices, a, units):
            send_native[devices, hh, a] = units

        for block in range(4):
            rows_to_units(lambda a: native.at[a], block, hh * HALF, put)

    pltpu.make_async_copy(send_native.at[me], got_qk.at[frame_at, half], qk_recv).start()

    each_near(
        lambda to: remote(
            send_native.at[to], got_qk.at[frame_at, half], native_send, qk_recv, to
        ).start()
    )

    @pl.loop(0, 2)
    def _(g):
        for a in range(3):
            own_copy(a, g).wait()
            trade_copy(a, g).wait_recv()

        @pl.when(g == 1)
        def _():
            def put_relay(devices, a, units):
                send_relay[devices, a] = units

            for block in range(4):
                rows_to_units(lambda a: frame.at[a, other], block, 0, put_relay)

            pltpu.make_async_copy(send_relay.at[me], got_qk.at[frame_at, other, half], qk_recv).start()

            each_near(
                lambda to: remote(
                    send_relay.at[to], got_qk.at[frame_at, other, half], relay_send, qk_recv, to
                ).start()
            )

        @pl.when(g == 0)
        def _():
            each_far(
                lambda to: remote(
                    send_native.at[to, half],
                    got_qk.at[frame_at, half, half],
                    native_send,
                    qk_recv,
                    to,
                ).start()
            )

        @pl.loop(0, 4)
        def _(h):
            columns = pl.ds(pl.multiple_of(g * PART + h * HD, HD), HD)
            q_hat, _ = hat(frame[0, :, :, columns].reshape(256, HD).astype(F32))
            k_hat, _ = hat(frame[1, :, :, columns].reshape(256, HD).astype(F32))
            q = (q_hat * gain[0]).astype(BF)
            k = (k_hat * gain[1]).astype(BF)
            weights = softmax(dot(q, k, NT))
            probs[g * 4 + h] = weights
            result = dot(weights.astype(BF), frame[2, :, :, columns].reshape(256, HD), NN)
            o_space[g, h] = result.astype(BF).reshape(2, 4, 32, HD)

        for b in range(4):
            moved = dot(select[0], o_space[g, :, :, b].reshape(256, HD), NN).astype(BF)
            send_o[g, pl.ds(b * 16, 16)] = moved.reshape(16, 16, HD)

        slot = g * 2 + half
        pltpu.make_async_copy(send_o.at[g, me], got_o.at[slot, frame_at], o_recv.at[slot]).start()

        each_peer(
            lambda to: remote(
                send_o.at[g, to], got_o.at[slot, frame_at], o_send.at[g], o_recv.at[slot], to
            ).start()
        )

    def send_cross(hh):
        for part in range(4):
            units = [time_dqk[hh, a, :, :, part].reshape(256, HD).astype(BF) for a in range(2)]
            moved = dot(select[7], jnp.concatenate(units, axis=1), NN).astype(BF)
            for a in range(2):
                send_dqk[hh, pl.ds(part * 8, 8), :, a] = moved[:, a * HD : (a + 1) * HD].reshape(
                    8, 2, 16, HD
                )
        own_kind = half if hh == 0 else 1 - half
        pltpu.make_async_copy(
            send_dqk.at[hh, frame_at, 1 - hh], got_cross.at[own_kind, me], cross_recv.at[own_kind]
        ).start()

        def send_one(to):
            side = ((y + 11 - 2 * (to % 4)) % 8) // 4
            kind = side if hh == 0 else 1 - side
            remote(
                send_dqk.at[hh, to, 1 - hh],
                got_cross.at[kind, me],
                cross_send,
                cross_recv.at[kind],
                to * 2 + side,
            ).start()

        each_frame(send_one)

    wait_bytes(got_qk, qk_recv)
    for hh in range(2):
        for part in range(4):
            here = pl.ds(part * 8, 8)
            units = [got_qk[here, :, hh, a].reshape(256, HD) for a in range(2)]
            moved = dot(select[6], jnp.concatenate(units, axis=1), NN)
            for a in range(2):
                time_qk[hh, a, :, :, part] = moved[:, a * HD : (a + 1) * HD].reshape(8, 4, 8, HD)

    mixed_in.wait()
    group = lax.broadcasted_iota(jnp.int32, (ROWS, ROWS), 0) // FRAMES
    same = group == lax.broadcasted_iota(jnp.int32, (ROWS, ROWS), 1) // FRAMES

    @pl.loop(0, 4)
    def _(t):
        hh = t % 2
        g = t // 2
        wait_bytes(got_o.at[t], o_recv.at[t])
        for part in range(2):
            units = got_o[t, pl.ds(part * 16, 16)].reshape(256, HD)
            time_o[:, :, part] = dot(select[2], units, NN).astype(BF).reshape(4, 4, 16, HD)

        heads = range(4)

        def each(one, *stacked):
            return jnp.concatenate(
                [one(*(values[h * ROWS : (h + 1) * ROWS] for values in stacked)) for h in heads], axis=0
            )

        columns = [
            pl.ds(pl.multiple_of(hh * HALF + g * PART + h * HD, HD), HD) for h in heads
        ]
        q_hat, q_factor = hat(time_qk[hh, 0, pl.ds(g * 4, 4)].reshape(4 * ROWS, HD))
        k_hat, k_factor = hat(time_qk[hh, 1, pl.ds(g * 4, 4)].reshape(4 * ROWS, HD))
        o = time_o[...].reshape(4 * ROWS, HD)
        q = (q_hat * gain[2]).astype(BF)
        k = (k_hat * gain[3]).astype(BF)
        scores = each(lambda q, k: jnp.where(same, dot(q, k, NT), -1e30), q, k)
        weights = softmax(scores)
        rounded = weights.astype(BF)
        result = each(lambda w, o: dot(w, o, NN), rounded, o).astype(BF)
        for h in heads:
            time_mixed[:, columns[h]] = result[h * ROWS : (h + 1) * ROWS]
        d_out = jnp.concatenate([d_time[:, columns[h]] for h in heads], axis=0)
        delta = jnp.sum(d_out.astype(F32) * result.astype(F32), axis=-1, keepdims=True)
        d_weights = each(lambda d, o: dot(d, o, NT), d_out, o)
        d_scores = (weights * (d_weights - delta) * SCALE).astype(BF)
        time_d[...] = (
            each(lambda w, d: dot(w, d, TN), rounded, d_out).astype(BF).reshape(4, 4, 2, 16, HD)
        )
        d_q, product = norm_back(
            q_hat, q_factor, gain[2], each(lambda s, k: dot(s, k, NN), d_scores, k)
        )
        sums[2] += fold(product)
        time_dqk[hh, 0, pl.ds(g * 4, 4)] = d_q.reshape(4, 4, 4, 8, HD)
        d_k, product = norm_back(
            k_hat, k_factor, gain[3], each(lambda s, q: dot(s, q, TN), d_scores, q)
        )
        sums[3] += fold(product)
        time_dqk[hh, 1, pl.ds(g * 4, 4)] = d_k.reshape(4, 4, 4, 8, HD)

        for part in range(2):
            moved = dot(select[3], time_d[:, :, part].reshape(256, HD), NN).astype(BF)
            send_d[t, pl.ds(part * 16, 16)] = moved.reshape(16, 16, HD)

        def send_one(to):
            remote(send_d.at[t, to], got_d.at[g, me], d_send, d_recv.at[g], to * 2 + hh).start()

        @pl.when(hh == half)
        def _():
            pltpu.make_async_copy(send_d.at[t, frame_at], got_d.at[g, me], d_recv.at[g]).start()

        @pl.when(hh != half)
        def _():
            send_one(frame_at)

        each_frame(send_one)

        @pl.when(t == 2)
        def _():
            send_cross(0)

    mixed_out = pltpu.make_async_copy(time_mixed, mixed, mixed_sem)
    mixed_out.start()

    send_cross(1)
    pltpu.make_async_copy(send_dqk.at[half, frame_at, half], got_own.at[me], back_recv).start()
    remote(
        send_dqk.at[other, frame_at, other], got_own.at[me], back_send, back_recv, partner
    ).start()

    def send_own(to):
        for hh in range(2):
            remote(
                send_dqk.at[hh, to, hh], got_own.at[me], back_send, back_recv, to * 2 + hh
            ).start()

    each_frame(send_own)

    def out_own(a, g):
        return pltpu.make_async_copy(
            final_own.at[a, :, pl.ds(g * PART, PART)],
            outputs[a].at[:, pl.ds(half * HALF + g * PART, PART)],
            out_sem.at[a, g],
        )

    def out_trade(a, g):
        place = half * HALF + g * PART
        target = value_grad.at[:, pl.ds(place, PART)] if a == 2 else final_in.at[a, :, pl.ds(g * PART, PART)]
        return remote(
            final_out.at[a, :, pl.ds(g * PART, PART)],
            target,
            out_send.at[a, g],
            out_recv.at[a, g],
            partner,
        )

    def units_to_rows(units, block):
        here = pl.ds(block * 16, 16)
        pieces = [units[here, a].reshape(256, HD) for a in range(2)]
        return dot(select[5], jnp.concatenate(pieces, axis=1), NN)

    @pl.loop(0, 2)
    def _(g):
        wait_bytes(got_d.at[g], d_recv.at[g])

        for b in range(4):
            moved = dot(select[1], got_d[g, pl.ds(b * 16, 16)].reshape(256, HD), NN).astype(BF)
            d_space[:, :, b] = moved.reshape(4, 2, 32, HD)

        @pl.loop(0, 4)
        def _(h):
            columns = pl.ds(pl.multiple_of(g * PART + h * HD, HD), HD)
            q_hat, q_factor = hat(frame[0, :, :, columns].reshape(256, HD).astype(F32))
            k_hat, k_factor = hat(frame[1, :, :, columns].reshape(256, HD).astype(F32))
            q = (q_hat * gain[0]).astype(BF)
            k = (k_hat * gain[1]).astype(BF)
            v = frame[2, :, :, columns].reshape(256, HD)
            weights = probs[g * 4 + h]
            d_out = d_space[h].reshape(256, HD)
            result = o_space[g, h].reshape(256, HD)
            delta = jnp.sum(d_out.astype(F32) * result.astype(F32), axis=-1, keepdims=True)
            d_scores = (weights * (dot(d_out, v, NT) - delta) * SCALE).astype(BF)
            d_q, product = norm_back(q_hat, q_factor, gain[0], dot(d_scores, k, NN))
            sums[0] += fold(product)
            back[0, g * 4 + h] = d_q.reshape(2, ROWS, HD)
            d_k, product = norm_back(k_hat, k_factor, gain[1], dot(d_scores, q, TN))
            sums[1] += fold(product)
            back[1, g * 4 + h] = d_k.reshape(2, ROWS, HD)
            d_v = dot(weights.astype(BF), d_out, TN).astype(BF).reshape(2, ROWS, HD)
            final_out[2, :, columns] = lax.select(half == 0, d_v[1], d_v[0])
            final_own[2, :, columns] = lax.select(half == 0, d_v[0], d_v[1])

        out_trade(2, g).start()
        out_own(2, g).start()

    def add_units(units, r, target):
        for block in range(4):
            moved = units_to_rows(units, block)
            here = pl.ds(block * 32, 32)
            for a in range(2):
                for h in range(8):
                    total = moved[h * 32 : h * 32 + 32, a * HD : (a + 1) * HD] + back[a, h, r, here]
                    target[a, here, h * HD : (h + 1) * HD] = total.astype(BF)

    rounds = (
        (y, lambda at: {"seq": z * 32 + x * 8 + at}),
        (z * 4 + x, lambda at: {"seq": at * 8 + y}),
        (sample, lambda at: {"dp": at}),
    )

    def gather(i, total):
        place, device = rounds[i]
        gathered[i, place] = total

        @pl.loop(1, 8)
        def _(step):
            remote(
                gathered.at[i, place],
                gathered.at[i, place],
                sum_send.at[i],
                sum_recv.at[i],
                device((place + step) % 8),
            ).start()

    def gathered_sum(i):
        wait_bytes(gathered.at[i, pl.ds(0, 7)], sum_recv.at[i])
        return jnp.sum(gathered[i], axis=0)

    own = jnp.sum(sums[...], axis=1)
    gather(0, jnp.concatenate([own, jnp.zeros_like(own)], axis=0))

    wait_bytes(got_cross.at[0, pl.ds(0, 32)], cross_recv.at[0])
    add_units(got_cross.at[0], other, final_out)
    gather(1, gathered_sum(0))
    for a in range(2):
        for g in range(2):
            out_trade(a, g).start()

    gather(2, gathered_sum(1))
    wait_bytes(got_own, back_recv)
    add_units(got_own, half, final_own)
    for g in range(2):
        for a in range(2):
            out_own(a, g).start()

    wait_bytes(got_cross.at[1, pl.ds(0, 32)], cross_recv.at[1])

    added = [units_to_rows(got_cross.at[1], block) for block in range(4)]
    for a in range(2):
        for g in range(2):
            out_trade(a, g).wait_recv()
        for block in range(4):
            here = pl.ds(block * 32, 32)
            for h in range(8):
                columns = slice(h * HD, (h + 1) * HD)
                place = pl.ds(pl.multiple_of(other * HALF + h * HD, HD), HD)
                total = added[block][h * 32 : h * 32 + 32, a * HD : (a + 1) * HD] + final_in[
                    a, here, columns
                ].astype(F32)
                outputs[a][here, place] = total.astype(BF)
    gain_grads[...] = gathered_sum(2)[0:4]

    for i in range(3):
        wait_bytes(gathered.at[i, pl.ds(0, 7)], sum_send.at[i])
    for g in range(2):
        out_trade(2, g).wait_recv()
        for a in range(3):
            trade_copy(a, g).wait_send()
            out_trade(a, g).wait_send()
            out_own(a, g).wait()
        wait_bytes(send_o.at[g, pl.ds(0, SEQ - 1)], o_send.at[g])
    wait_bytes(send_native.at[pl.ds(0, 47)], native_send)
    wait_bytes(send_relay.at[pl.ds(0, 31)], relay_send)
    wait_bytes(got_d.at[:, pl.ds(0, SEQ - 1)], d_send)
    wait_bytes(got_cross.at[:, pl.ds(0, 31)], cross_send)
    wait_bytes(got_own.at[pl.ds(0, 63)], back_send)
    mixed_out.wait()


def write_out(*refs):
    sources, targets, sem = refs[:5], refs[5:10], refs[10]
    copies = [
        pltpu.make_async_copy(source, target, sem.at[i])
        for i, (source, target) in enumerate(zip(sources, targets))
    ]
    for copy in copies:
        copy.start()
    for copy in copies:
        copy.wait()


def body(query, key, value, gains, d_mixed):
    wide = (ROWS, WIDTH)
    hbm_spec = pl.BlockSpec(memory_space=pltpu.HBM)
    any_spec = pl.BlockSpec(memory_space=pl.ANY)
    vmem_spec = pl.BlockSpec(memory_space=pltpu.VMEM)
    dma = pltpu.SemaphoreType.DMA
    shapes = [jax.ShapeDtypeStruct(wide, BF)] * 4 + [jax.ShapeDtypeStruct((4, HD), F32)]
    results = pl.pallas_call(
        kernel,
        out_shape=shapes,
        in_specs=[hbm_spec] * 5,
        out_specs=[vmem_spec] * 5,
        scratch_shapes=[
            pltpu.VMEM((4, HD), F32),
            pltpu.VMEM((len(SELECTORS), 256, 256), BF),
            pltpu.VMEM((2, ROWS, WIDTH), BF),
            pltpu.VMEM((3, 2, ROWS, HALF), BF),
            pltpu.VMEM(wide, BF),
            pltpu.VMEM((8, 256, 256), F32),
            pltpu.VMEM((2, 4, 2, 4, 32, HD), BF),
            pltpu.VMEM((SEQ, 2, 2, 16, HD), BF),
            pltpu.VMEM((SEQ, 2, 16, HD), BF),
            pltpu.VMEM((2, SEQ, 16, HD), BF),
            pltpu.VMEM((FRAMES, 2, 2, 2, 16, HD), BF),
            pltpu.VMEM((4, FRAMES, 16, HD), BF),
            pltpu.VMEM((2, 2, 8, 4, 4, 8, HD), F32),
            pltpu.VMEM((4, 4, 2, 16, HD), BF),
            pltpu.VMEM((4, 4, 2, 16, HD), BF),
            pltpu.VMEM((2, 2, 8, 4, 4, 8, HD), F32),
            pltpu.VMEM(wide, BF),
            pltpu.VMEM((4, FRAMES, 16, HD), BF),
            pltpu.VMEM((2, FRAMES, 2, 2, 16, HD), BF),
            pltpu.VMEM((2, SEQ, 16, HD), BF),
            pltpu.VMEM((SEQ, 2, 16, HD), BF),
            pltpu.VMEM((2, SEQ, 2, 16, HD), BF),
            pltpu.VMEM((4, 2, 4, 32, HD), BF),
            pltpu.VMEM((2, 8, 2, ROWS, HD), F32),
            pltpu.VMEM((3, ROWS, HALF), BF),
            pltpu.VMEM((3, ROWS, HALF), BF),
            pltpu.VMEM((2, ROWS, HALF), BF),
            pltpu.VMEM((4, 8, HD), F32),
            pltpu.VMEM((3, 8, 8, HD), F32),
            dma,
            dma((2,)),
            dma((3, 2)),
            dma((3, 2)),
            dma((3, 2)),
            dma,
            dma,
            dma,
            dma,
            dma,
            dma((2,)),
            dma((4,)),
            dma,
            dma((2,)),
            dma,
            dma,
            dma((2,)),
            dma,
            dma((3, 2)),
            dma((3, 2)),
            dma((3, 2)),
            dma((3,)),
            dma((3,)),
        ],
        compiler_params=pltpu.CompilerParams(
            collective_id=0, has_side_effects=True, vmem_limit_bytes=103 * 2**19
        ),
        cost_estimate=pl.CostEstimate(flops=2 * 10**9, bytes_accessed=2**22, transcendentals=10**6),
        name="space_time_attention",
    )(query.reshape(wide), key.reshape(wide), value.reshape(wide), gains, d_mixed.reshape(wide))
    mixed, query_grad, key_grad, value_grad, gain_grads = pl.pallas_call(
        write_out,
        out_shape=shapes,
        in_specs=[vmem_spec] * 5,
        out_specs=[hbm_spec] * 5,
        scratch_shapes=[dma((5,))],
        compiler_params=pltpu.CompilerParams(vmem_limit_bytes=4 * 2**20),
        name="write_out",
    )(*results)
    return (
        mixed.reshape(d_mixed.shape),
        query_grad.reshape(query.shape),
        key_grad.reshape(key.shape),
        value_grad.reshape(value.shape),
        gain_grads,
    )


def solution(mesh):
    placed = (
        P("dp", "seq", None),
        P("dp", "seq", None),
        P("dp", "seq", None),
        P(),
        P("dp", None, "seq", None, None),
    )
    return jax.shard_map(
        body,
        mesh=mesh,
        in_specs=placed,
        out_specs=(
            P("dp", None, "seq", None, None),
            P("dp", "seq", None),
            P("dp", "seq", None),
            P("dp", "seq", None),
            P(),
        ),
        check_vma=False,
    )
```

```python
import jax
import jax.numpy as jnp
from jax import lax
from jax.experimental import pallas as pl
from jax.experimental.pallas import tpu as pltpu
from jax.sharding import PartitionSpec as P

SEQ = 64
DP = 8
WIDTH = 2048
HALF = 1024
PART = 512
HD = 128
ROWS = 128
FRAMES = 32
EPS = 1e-06
SCALE = HD**-0.5
SCALE2 = SCALE * 1.4426950408889634
BF = jnp.bfloat16
F32 = jnp.float32


def dot(a, b, dims):
    return lax.dot_general(a, b, (dims, ((), ())), preferred_element_type=F32)


NN = ((1,), (0,))
NT = ((1,), (1,))
TN = ((0,), (0,))


def selector(column_of_row):
    row = lax.broadcasted_iota(jnp.int32, (256, 256), 0)
    column = lax.broadcasted_iota(jnp.int32, (256, 256), 1)
    return jnp.where(column == column_of_row(row), 1.0, 0.0).astype(BF)


def from_space(o):
    return (o & 3) * 64 + ((o >> 2) & 1) * 32 + (o >> 4) * 2 + ((o >> 3) & 1)


def to_space(i):
    return ((i & 31) >> 1) * 16 + (i & 1) * 8 + ((i >> 5) & 1) * 4 + (i >> 6)


def to_time(o):
    return (o & 15) * 16 + ((o >> 4) & 1) * 8 + ((o >> 5) & 1) * 4 + (o >> 6)


def from_time(i):
    return (i & 3) * 64 + (((i >> 2) & 1) * 2 + ((i >> 3) & 1)) * 16 + (i >> 4)


def from_rows(o):
    return (o & 7) * 32 + (o >> 4) * 2 + ((o >> 3) & 1)


def to_rows(i):
    return ((i & 31) >> 1) * 16 + (i & 1) * 8 + (i >> 5)


def to_time8(o):
    return (o & 7) * 32 + ((o >> 4) & 1) * 16 + ((o >> 3) & 1) * 8 + (o >> 5)


def from_time8(c):
    return (c & 7) * 32 + (((c >> 4) & 1) * 2 + ((c >> 3) & 1)) * 8 + (c >> 5)


SELECTORS = (from_space, to_space, to_time, from_time, from_rows, to_rows, to_time8, from_time8)


def hat(values):
    factor = lax.rsqrt(jnp.sum(values * values, axis=-1, keepdims=True) * (1.0 / HD) + EPS)
    return values * factor, factor


def softmax(scores):
    peak = jnp.max(scores, axis=-1, keepdims=True)
    raised = jnp.exp2((scores - peak) * SCALE2)
    return raised * (1.0 / jnp.sum(raised, axis=-1, keepdims=True))


def norm_back(x_hat, factor, gain, incoming):
    product = incoming * x_hat
    mean = jnp.sum(product * gain, axis=-1, keepdims=True) * (1.0 / HD)
    return factor * (incoming * gain - x_hat * mean), product


def fold(product):
    return jnp.sum(product.reshape(-1, 8, HD), axis=0)


def kernel(
    query, key, value, gains_in, d_mixed,
    mixed, query_grad, key_grad, value_grad, gain_grads,
    gains, select, native, frame, d_time, probs, o_space, send_native, send_relay, send_o, got_qk, got_o,
    time_qk, time_o, time_d, time_dqk, time_mixed, send_d, send_dqk, got_d, got_own, got_cross,
    d_space, back, final_out, final_own, final_in, sums, gathered,
    gains_sem, native_sem, own_sem, trade_send, trade_recv, mixed_in_sem, mixed_sem,
    native_send, relay_send, qk_recv, o_send, o_recv, d_send, d_recv,
    cross_send, back_send, cross_recv, back_recv,
    out_sem, out_send, out_recv, sum_send, sum_recv,
):
    me = lax.axis_index("seq")
    sample = lax.axis_index("dp")
    z, x, y = me // 32, (me // 8) % 4, me % 8
    half, frame_at = me % 2, me // 2
    other = 1 - half
    partner = me + 1 - 2 * half

    def each_peer(one):
        @pl.loop(1, 8)
        def _(at):
            base = ((z + (8 - at) // 4) % 2) * 32 + ((x + (8 - at) % 4) % 4) * 8
            for dy in (4, 3, 5, 2, 6, 1, 7, 0):
                one(base + (y + dy) % 8)

        for dy in (4, 3, 5, 2, 6, 1, 7):
            one(z * 32 + x * 8 + (y + dy) % 8)

    def each_frame(one):
        @pl.loop(1, 8)
        def _(at):
            base = ((z + (8 - at) // 4) % 2) * 16 + ((x + (8 - at) % 4) % 4) * 4
            for dy in (2, 1, 3, 0):
                one(base + (y // 2 + dy) % 4)

        for dy in (2, 1, 3):
            one(z * 16 + x * 4 + (y // 2 + dy) % 4)

    away = 2 * half - 1

    def each_near(one):
        @pl.loop(1, 8)
        def _(at):
            base = ((z + (8 - at) // 4) % 2) * 32 + ((x + (8 - at) % 4) % 4) * 8
            for dy in (3, 2, 1, 0):
                one(base + (y + 8 + dy * away) % 8)

        for dy in (3, 2, 1):
            one(z * 32 + x * 8 + (y + 8 + dy * away) % 8)

    def each_far(one):
        @pl.loop(0, 8)
        def _(at):
            base = ((z + (7 - at) // 4) % 2) * 32 + ((x + (7 - at) % 4) % 4) * 8
            for dy in (4, 3, 2, 1):
                one(base + (y + 8 - dy * away) % 8)

    def remote(source, target, send_sem, recv_sem, to):
        return pltpu.make_async_remote_copy(
            src_ref=source,
            dst_ref=target,
            send_sem=send_sem,
            recv_sem=recv_sem,
            device_id=to if isinstance(to, dict) else {"seq": to},
            device_id_type=pl.DeviceIdType.MESH,
        )

    def wait_bytes(ref, sem):
        pltpu.make_async_copy(ref, ref, sem).wait()

    inputs = (query, key, value)
    outputs = (query_grad, key_grad, value_grad)

    def own_copy(a, g):
        return pltpu.make_async_copy(
            inputs[a].at[:, pl.ds(half * HALF + g * PART, PART)],
            frame.at[a, half, :, pl.ds(g * PART, PART)],
            own_sem.at[a, g],
        )

    def trade_copy(a, g):
        return remote(
            inputs[a].at[:, pl.ds(other * HALF + g * PART, PART)],
            frame.at[a, half, :, pl.ds(g * PART, PART)],
            trade_send.at[a, g],
            trade_recv.at[a, g],
            partner,
        )

    gains_copy = pltpu.make_async_copy(gains_in, gains, gains_sem)
    gains_copy.start()
    native_copies = [
        pltpu.make_async_copy(inputs[a], native.at[a], native_sem.at[a]) for a in range(2)
    ]
    for copy in native_copies:
        copy.start()
    for g in range(2):
        for a in range(3):
            own_copy(a, g).start()
    mixed_in = pltpu.make_async_copy(d_mixed, d_time, mixed_in_sem)
    mixed_in.start()
    got_cross[...] = jnp.zeros_like(got_cross)

    barrier = pltpu.get_barrier_semaphore()

    @pl.loop(1, DP)
    def _(step):
        pl.semaphore_signal(
            barrier,
            inc=1,
            device_id={"dp": (sample + step) % DP},
            device_id_type=pl.DeviceIdType.MESH,
        )

    each_peer(
        lambda to: pl.semaphore_signal(
            barrier, inc=1, device_id={"seq": to}, device_id_type=pl.DeviceIdType.MESH
        )
    )

    pl.semaphore_wait(barrier, SEQ - 1 + DP - 1)

    for g in range(2):
        for a in range(3):
            trade_copy(a, g).start()

    for i, source in enumerate(SELECTORS):
        select[i] = selector(source)
    sums[...] = jnp.zeros_like(sums)
    gains_copy.wait()
    gain = [gains[i : i + 1, :] for i in range(4)]

    def rows_to_units(source, block, first, target):
        pieces = [
            jnp.concatenate(
                [source(a)[pl.ds(block * 32, 32), pl.ds(first + h * HD, HD)] for h in range(8)], axis=0
            )
            for a in range(2)
        ]
        moved = dot(select[4], jnp.concatenate(pieces, axis=1), NN).astype(BF)
        for a in range(2):
            target(pl.ds(block * 16, 16), a, moved[:, a * HD : (a + 1) * HD].reshape(16, 16, HD))

    for copy in native_copies:
        copy.wait()

    for hh in range(2):

        def put(devices, a, units):
            send_native[devices, hh, a] = units

        for block in range(4):
            rows_to_units(lambda a: native.at[a], block, hh * HALF, put)

    pltpu.make_async_copy(send_native.at[me], got_qk.at[frame_at, half], qk_recv).start()

    each_near(
        lambda to: remote(
            send_native.at[to], got_qk.at[frame_at, half], native_send, qk_recv, to
        ).start()
    )

    def two_at_once(one_head):
        @pl.loop(0, 2)
        def _(pair):
            one_head(pair * 2)
            one_head(pair * 2 + 1)

    @pl.loop(0, 2)
    def _(g):
        for a in range(3):
            own_copy(a, g).wait()
            trade_copy(a, g).wait_recv()

        @pl.when(g == 1)
        def _():
            def put_relay(devices, a, units):
                send_relay[devices, a] = units

            for block in range(4):
                rows_to_units(lambda a: frame.at[a, other], block, 0, put_relay)

            pltpu.make_async_copy(send_relay.at[me], got_qk.at[frame_at, other, half], qk_recv).start()

            each_near(
                lambda to: remote(
                    send_relay.at[to], got_qk.at[frame_at, other, half], relay_send, qk_recv, to
                ).start()
            )

        @pl.when(g == 0)
        def _():
            each_far(
                lambda to: remote(
                    send_native.at[to, half],
                    got_qk.at[frame_at, half, half],
                    native_send,
                    qk_recv,
                    to,
                ).start()
            )

        @two_at_once
        def _(h):
            columns = pl.ds(pl.multiple_of(g * PART + h * HD, HD), HD)
            q_hat, _ = hat(frame[0, :, :, columns].reshape(256, HD).astype(F32))
            k_hat, _ = hat(frame[1, :, :, columns].reshape(256, HD).astype(F32))
            q = (q_hat * gain[0]).astype(BF)
            k = (k_hat * gain[1]).astype(BF)
            weights = softmax(dot(q, k, NT))
            probs[g * 4 + h] = weights
            result = dot(weights.astype(BF), frame[2, :, :, columns].reshape(256, HD), NN)
            o_space[g, h] = result.astype(BF).reshape(2, 4, 32, HD)

        for b in range(4):
            moved = dot(select[0], o_space[g, :, :, b].reshape(256, HD), NN).astype(BF)
            send_o[g, pl.ds(b * 16, 16)] = moved.reshape(16, 16, HD)

        slot = g * 2 + half
        pltpu.make_async_copy(send_o.at[g, me], got_o.at[slot, frame_at], o_recv.at[slot]).start()

        each_peer(
            lambda to: remote(
                send_o.at[g, to], got_o.at[slot, frame_at], o_send.at[g], o_recv.at[slot], to
            ).start()
        )

    def send_cross(hh):
        for part in range(4):
            units = [time_dqk[hh, a, :, :, part].reshape(256, HD).astype(BF) for a in range(2)]
            moved = dot(select[7], jnp.concatenate(units, axis=1), NN).astype(BF)
            for a in range(2):
                send_dqk[hh, pl.ds(part * 8, 8), :, a] = moved[:, a * HD : (a + 1) * HD].reshape(
                    8, 2, 16, HD
                )
        own_kind = half if hh == 0 else 1 - half
        pltpu.make_async_copy(
            send_dqk.at[hh, frame_at, 1 - hh], got_cross.at[own_kind, me], cross_recv.at[own_kind]
        ).start()

        def send_one(to):
            side = ((y + 11 - 2 * (to % 4)) % 8) // 4
            kind = side if hh == 0 else 1 - side
            remote(
                send_dqk.at[hh, to, 1 - hh],
                got_cross.at[kind, me],
                cross_send,
                cross_recv.at[kind],
                to * 2 + side,
            ).start()

        each_frame(send_one)

    wait_bytes(got_qk, qk_recv)
    for hh in range(2):
        for part in range(4):
            here = pl.ds(part * 8, 8)
            units = [got_qk[here, :, hh, a].reshape(256, HD) for a in range(2)]
            moved = dot(select[6], jnp.concatenate(units, axis=1), NN)
            for a in range(2):
                time_qk[hh, a, :, :, part] = moved[:, a * HD : (a + 1) * HD].reshape(8, 4, 8, HD)

    mixed_in.wait()
    group = lax.broadcasted_iota(jnp.int32, (ROWS, ROWS), 0) // FRAMES
    same = group == lax.broadcasted_iota(jnp.int32, (ROWS, ROWS), 1) // FRAMES

    @pl.loop(0, 4)
    def _(t):
        hh = t % 2
        g = t // 2
        wait_bytes(got_o.at[t], o_recv.at[t])
        for part in range(2):
            units = got_o[t, pl.ds(part * 16, 16)].reshape(256, HD)
            time_o[:, :, part] = dot(select[2], units, NN).astype(BF).reshape(4, 4, 16, HD)

        heads = range(4)

        def each(one, *stacked):
            return jnp.concatenate(
                [one(*(values[h * ROWS : (h + 1) * ROWS] for values in stacked)) for h in heads], axis=0
            )

        columns = [
            pl.ds(pl.multiple_of(hh * HALF + g * PART + h * HD, HD), HD) for h in heads
        ]
        q_hat, q_factor = hat(time_qk[hh, 0, pl.ds(g * 4, 4)].reshape(4 * ROWS, HD))
        k_hat, k_factor = hat(time_qk[hh, 1, pl.ds(g * 4, 4)].reshape(4 * ROWS, HD))
        o = time_o[...].reshape(4 * ROWS, HD)
        q = (q_hat * gain[2]).astype(BF)
        k = (k_hat * gain[3]).astype(BF)
        scores = each(lambda q, k: jnp.where(same, dot(q, k, NT), -1e30), q, k)
        weights = softmax(scores)
        rounded = weights.astype(BF)
        result = each(lambda w, o: dot(w, o, NN), rounded, o).astype(BF)
        for h in heads:
            time_mixed[:, columns[h]] = result[h * ROWS : (h + 1) * ROWS]
        d_out = jnp.concatenate([d_time[:, columns[h]] for h in heads], axis=0)
        delta = jnp.sum(d_out.astype(F32) * result.astype(F32), axis=-1, keepdims=True)
        d_weights = each(lambda d, o: dot(d, o, NT), d_out, o)
        d_scores = (weights * (d_weights - delta) * SCALE).astype(BF)
        time_d[...] = (
            each(lambda w, d: dot(w, d, TN), rounded, d_out).astype(BF).reshape(4, 4, 2, 16, HD)
        )
        d_q, product = norm_back(
            q_hat, q_factor, gain[2], each(lambda s, k: dot(s, k, NN), d_scores, k)
        )
        sums[2] += fold(product)
        time_dqk[hh, 0, pl.ds(g * 4, 4)] = d_q.reshape(4, 4, 4, 8, HD)
        d_k, product = norm_back(
            k_hat, k_factor, gain[3], each(lambda s, q: dot(s, q, TN), d_scores, q)
        )
        sums[3] += fold(product)
        time_dqk[hh, 1, pl.ds(g * 4, 4)] = d_k.reshape(4, 4, 4, 8, HD)

        for part in range(2):
            moved = dot(select[3], time_d[:, :, part].reshape(256, HD), NN).astype(BF)
            send_d[t, pl.ds(part * 16, 16)] = moved.reshape(16, 16, HD)

        def send_one(to):
            remote(send_d.at[t, to], got_d.at[g, me], d_send, d_recv.at[g], to * 2 + hh).start()

        @pl.when(hh == half)
        def _():
            pltpu.make_async_copy(send_d.at[t, frame_at], got_d.at[g, me], d_recv.at[g]).start()

        @pl.when(hh != half)
        def _():
            send_one(frame_at)

        each_frame(send_one)

        @pl.when(t == 2)
        def _():
            send_cross(0)

    mixed_out = pltpu.make_async_copy(time_mixed, mixed, mixed_sem)
    mixed_out.start()

    send_cross(1)
    pltpu.make_async_copy(send_dqk.at[half, frame_at, half], got_own.at[me], back_recv).start()
    remote(
        send_dqk.at[other, frame_at, other], got_own.at[me], back_send, back_recv, partner
    ).start()

    def send_own(to):
        for hh in range(2):
            remote(
                send_dqk.at[hh, to, hh], got_own.at[me], back_send, back_recv, to * 2 + hh
            ).start()

    each_frame(send_own)

    def out_own(a, g):
        return pltpu.make_async_copy(
            final_own.at[a, :, pl.ds(g * PART, PART)],
            outputs[a].at[:, pl.ds(half * HALF + g * PART, PART)],
            out_sem.at[a, g],
        )

    def out_trade(a, g):
        place = half * HALF + g * PART
        target = value_grad.at[:, pl.ds(place, PART)] if a == 2 else final_in.at[a, :, pl.ds(g * PART, PART)]
        return remote(
            final_out.at[a, :, pl.ds(g * PART, PART)],
            target,
            out_send.at[a, g],
            out_recv.at[a, g],
            partner,
        )

    def units_to_rows(units, block):
        here = pl.ds(block * 16, 16)
        pieces = [units[here, a].reshape(256, HD) for a in range(2)]
        return dot(select[5], jnp.concatenate(pieces, axis=1), NN)

    @pl.loop(0, 2)
    def _(g):
        wait_bytes(got_d.at[g], d_recv.at[g])

        for b in range(4):
            moved = dot(select[1], got_d[g, pl.ds(b * 16, 16)].reshape(256, HD), NN).astype(BF)
            d_space[:, :, b] = moved.reshape(4, 2, 32, HD)

        @two_at_once
        def _(h):
            columns = pl.ds(pl.multiple_of(g * PART + h * HD, HD), HD)
            q_hat, q_factor = hat(frame[0, :, :, columns].reshape(256, HD).astype(F32))
            k_hat, k_factor = hat(frame[1, :, :, columns].reshape(256, HD).astype(F32))
            q = (q_hat * gain[0]).astype(BF)
            k = (k_hat * gain[1]).astype(BF)
            v = frame[2, :, :, columns].reshape(256, HD)
            weights = probs[g * 4 + h]
            d_out = d_space[h].reshape(256, HD)
            result = o_space[g, h].reshape(256, HD)
            delta = jnp.sum(d_out.astype(F32) * result.astype(F32), axis=-1, keepdims=True)
            d_scores = (weights * (dot(d_out, v, NT) - delta) * SCALE).astype(BF)
            d_q, product = norm_back(q_hat, q_factor, gain[0], dot(d_scores, k, NN))
            sums[0] += fold(product)
            back[0, g * 4 + h] = d_q.reshape(2, ROWS, HD)
            d_k, product = norm_back(k_hat, k_factor, gain[1], dot(d_scores, q, TN))
            sums[1] += fold(product)
            back[1, g * 4 + h] = d_k.reshape(2, ROWS, HD)
            d_v = dot(weights.astype(BF), d_out, TN).astype(BF).reshape(2, ROWS, HD)
            final_out[2, :, columns] = lax.select(half == 0, d_v[1], d_v[0])
            final_own[2, :, columns] = lax.select(half == 0, d_v[0], d_v[1])

        out_trade(2, g).start()
        out_own(2, g).start()

    def add_units(units, r, target):
        for block in range(4):
            moved = units_to_rows(units, block)
            here = pl.ds(block * 32, 32)
            for a in range(2):
                for h in range(8):
                    total = moved[h * 32 : h * 32 + 32, a * HD : (a + 1) * HD] + back[a, h, r, here]
                    target[a, here, h * HD : (h + 1) * HD] = total.astype(BF)

    rounds = (
        (y, lambda at: {"seq": z * 32 + x * 8 + at}),
        (z * 4 + x, lambda at: {"seq": at * 8 + y}),
        (sample, lambda at: {"dp": at}),
    )

    def gather(i, total):
        place, device = rounds[i]
        gathered[i, place] = total

        @pl.loop(1, 8)
        def _(step):
            remote(
                gathered.at[i, place],
                gathered.at[i, place],
                sum_send.at[i],
                sum_recv.at[i],
                device((place + step) % 8),
            ).start()

    def gathered_sum(i):
        wait_bytes(gathered.at[i, pl.ds(0, 7)], sum_recv.at[i])
        return jnp.sum(gathered[i], axis=0)

    own = jnp.sum(sums[...], axis=1)
    gather(0, jnp.concatenate([own, jnp.zeros_like(own)], axis=0))

    wait_bytes(got_cross.at[0, pl.ds(0, 32)], cross_recv.at[0])
    add_units(got_cross.at[0], other, final_out)
    gather(1, gathered_sum(0))
    for a in range(2):
        for g in range(2):
            out_trade(a, g).start()

    gather(2, gathered_sum(1))
    wait_bytes(got_own, back_recv)
    add_units(got_own, half, final_own)
    for g in range(2):
        for a in range(2):
            out_own(a, g).start()

    wait_bytes(got_cross.at[1, pl.ds(0, 32)], cross_recv.at[1])

    added = [units_to_rows(got_cross.at[1], block) for block in range(4)]
    for a in range(2):
        for g in range(2):
            out_trade(a, g).wait_recv()
        for block in range(4):
            here = pl.ds(block * 32, 32)
            for h in range(8):
                columns = slice(h * HD, (h + 1) * HD)
                place = pl.ds(pl.multiple_of(other * HALF + h * HD, HD), HD)
                total = added[block][h * 32 : h * 32 + 32, a * HD : (a + 1) * HD] + final_in[
                    a, here, columns
                ].astype(F32)
                outputs[a][here, place] = total.astype(BF)
    gain_grads[...] = gathered_sum(2)[0:4]

    for i in range(3):
        wait_bytes(gathered.at[i, pl.ds(0, 7)], sum_send.at[i])
    for g in range(2):
        out_trade(2, g).wait_recv()
        for a in range(3):
            trade_copy(a, g).wait_send()
            out_trade(a, g).wait_send()
            out_own(a, g).wait()
        wait_bytes(send_o.at[g, pl.ds(0, SEQ - 1)], o_send.at[g])
    wait_bytes(send_native.at[pl.ds(0, 47)], native_send)
    wait_bytes(send_relay.at[pl.ds(0, 31)], relay_send)
    wait_bytes(got_d.at[:, pl.ds(0, SEQ - 1)], d_send)
    wait_bytes(got_cross.at[:, pl.ds(0, 31)], cross_send)
    wait_bytes(got_own.at[pl.ds(0, 63)], back_send)
    mixed_out.wait()


def write_out(*refs):
    sources, targets, sem = refs[:5], refs[5:10], refs[10]
    copies = [
        pltpu.make_async_copy(source, target, sem.at[i])
        for i, (source, target) in enumerate(zip(sources, targets))
    ]
    for copy in copies:
        copy.start()
    for copy in copies:
        copy.wait()


def body(query, key, value, gains, d_mixed):
    wide = (ROWS, WIDTH)
    hbm_spec = pl.BlockSpec(memory_space=pltpu.HBM)
    any_spec = pl.BlockSpec(memory_space=pl.ANY)
    vmem_spec = pl.BlockSpec(memory_space=pltpu.VMEM)
    dma = pltpu.SemaphoreType.DMA
    shapes = [jax.ShapeDtypeStruct(wide, BF)] * 4 + [jax.ShapeDtypeStruct((4, HD), F32)]
    results = pl.pallas_call(
        kernel,
        out_shape=shapes,
        in_specs=[hbm_spec] * 5,
        out_specs=[vmem_spec] * 5,
        scratch_shapes=[
            pltpu.VMEM((4, HD), F32),
            pltpu.VMEM((len(SELECTORS), 256, 256), BF),
            pltpu.VMEM((2, ROWS, WIDTH), BF),
            pltpu.VMEM((3, 2, ROWS, HALF), BF),
            pltpu.VMEM(wide, BF),
            pltpu.VMEM((8, 256, 256), F32),
            pltpu.VMEM((2, 4, 2, 4, 32, HD), BF),
            pltpu.VMEM((SEQ, 2, 2, 16, HD), BF),
            pltpu.VMEM((SEQ, 2, 16, HD), BF),
            pltpu.VMEM((2, SEQ, 16, HD), BF),
            pltpu.VMEM((FRAMES, 2, 2, 2, 16, HD), BF),
            pltpu.VMEM((4, FRAMES, 16, HD), BF),
            pltpu.VMEM((2, 2, 8, 4, 4, 8, HD), F32),
            pltpu.VMEM((4, 4, 2, 16, HD), BF),
            pltpu.VMEM((4, 4, 2, 16, HD), BF),
            pltpu.VMEM((2, 2, 8, 4, 4, 8, HD), F32),
            pltpu.VMEM(wide, BF),
            pltpu.VMEM((4, FRAMES, 16, HD), BF),
            pltpu.VMEM((2, FRAMES, 2, 2, 16, HD), BF),
            pltpu.VMEM((2, SEQ, 16, HD), BF),
            pltpu.VMEM((SEQ, 2, 16, HD), BF),
            pltpu.VMEM((2, SEQ, 2, 16, HD), BF),
            pltpu.VMEM((4, 2, 4, 32, HD), BF),
            pltpu.VMEM((2, 8, 2, ROWS, HD), F32),
            pltpu.VMEM((3, ROWS, HALF), BF),
            pltpu.VMEM((3, ROWS, HALF), BF),
            pltpu.VMEM((2, ROWS, HALF), BF),
            pltpu.VMEM((4, 8, HD), F32),
            pltpu.VMEM((3, 8, 8, HD), F32),
            dma,
            dma((2,)),
            dma((3, 2)),
            dma((3, 2)),
            dma((3, 2)),
            dma,
            dma,
            dma,
            dma,
            dma,
            dma((2,)),
            dma((4,)),
            dma,
            dma((2,)),
            dma,
            dma,
            dma((2,)),
            dma,
            dma((3, 2)),
            dma((3, 2)),
            dma((3, 2)),
            dma((3,)),
            dma((3,)),
        ],
        compiler_params=pltpu.CompilerParams(
            collective_id=0, has_side_effects=True, vmem_limit_bytes=103 * 2**19
        ),
        cost_estimate=pl.CostEstimate(flops=2 * 10**9, bytes_accessed=2**22, transcendentals=10**6),
        name="space_time_attention",
    )(query.reshape(wide), key.reshape(wide), value.reshape(wide), gains, d_mixed.reshape(wide))
    mixed, query_grad, key_grad, value_grad, gain_grads = pl.pallas_call(
        write_out,
        out_shape=shapes,
        in_specs=[vmem_spec] * 5,
        out_specs=[hbm_spec] * 5,
        scratch_shapes=[dma((5,))],
        compiler_params=pltpu.CompilerParams(vmem_limit_bytes=4 * 2**20),
        name="write_out",
    )(*results)
    return (
        mixed.reshape(d_mixed.shape),
        query_grad.reshape(query.shape),
        key_grad.reshape(key.shape),
        value_grad.reshape(value.shape),
        gain_grads,
    )


def solution(mesh):
    placed = (
        P("dp", "seq", None),
        P("dp", "seq", None),
        P("dp", "seq", None),
        P(),
        P("dp", None, "seq", None, None),
    )
    return jax.shard_map(
        body,
        mesh=mesh,
        in_specs=placed,
        out_specs=(
            P("dp", None, "seq", None, None),
            P("dp", "seq", None),
            P("dp", "seq", None),
            P("dp", "seq", None),
            P(),
        ),
        check_vma=False,
    )
```
